512 devices in a mesh: rows: 128 (over y, z, core), sub: 4 (over x).
Axes of the slice: x: 4, y: 8, z: 8, core: 2. Of those that a mesh axis runs over, the one named last changes fastest.
Arguments:
- slab: float32 [131072, 1024], P(('rows', 'sub')), may hold values from -150 to 150
- test_matrix: float32 [1024, 72], replicated, may hold values from -6 to 6
Outputs:
- row_factor: float32 [131072, 72], P(('rows', 'sub'))
- projected: float32 [72, 1024], replicated
The draws below stay inside these ranges and needn't reach their ends.
All inputs are finite; a program needn't handle non-finite values.
Results may differ from the reference program's by a relative error of at most 0.0001.
Values sent between devices are 32-bit elements; how exact they have to be, the bound alone decides.
No kernel may reach another device: no remote copies, remote signals or barrier semaphores. Data moves between devices by JAX's collectives and lax.ppermute only.
A program may use at most 64 MiB of HBM per device.

```python
import math
import jax
import jax.numpy as jnp
from jax import lax

D = 1024
K = 72
ITERS = 2
TOTAL = 131072


def draw_slab(key, part):
    key = jax.random.fold_in(key, 11)
    first, second, third = jax.random.split(key, 3)
    base = jnp.clip(jax.random.normal(first, (TOTAL, D), jnp.float32), -6.0, 6.0)
    columns = jnp.exp(jax.random.uniform(second, (D,), jnp.float32, 0.0, math.log(10.0)))
    rowscale = jnp.exp(jax.random.uniform(third, (TOTAL, 1), jnp.float32, 0.0, math.log(10.0)))
    return base * rowscale * columns[None, :] / 4.0


def noise(stream_key, shape, spread, most, kind=jnp.bfloat16):
    drawn = spread * jax.random.normal(stream_key, shape, jnp.float32)
    return jnp.clip(drawn, min=-most, max=most).astype(kind)


def setup_inputs(seed: int = 0) -> dict:
    streams_of = jax.random.split(jax.random.key(seed), 3)
    slab = draw_slab(jax.random.fold_in(streams_of[2], 71), 0)
    test_matrix = noise(streams_of[1], (D, K), 1.0, 6.0, jnp.float32)
    return dict(slab=slab, test_matrix=test_matrix)


HI = lax.Precision.HIGHEST

def inverse_factor(gram):
    low = jnp.linalg.cholesky(gram)
    eye = jnp.eye(gram.shape[0], dtype=jnp.float32)
    return lax.linalg.triangular_solve(low, eye, left_side=True, lower=True)

def orthonormal(block):
    gram = jnp.dot(block.T, block, precision=HI)
    return jnp.dot(block, inverse_factor(gram).T, precision=HI)

def reference(slab, test_matrix):
    scale = math.sqrt(TOTAL)
    current = test_matrix
    for step in range(ITERS + 1):
        factor = orthonormal(jnp.dot(slab, current, precision=HI))
        cross = jnp.einsum('md,mk->dk', slab, factor, precision=HI)
        if step < ITERS:
            current = orthonormal(cross)
    return (factor * scale, cross.T / scale)
```

```python
import functools
import math

import jax
import jax.numpy as jnp
from jax import lax
from jax.experimental import pallas as pl
from jax.experimental.pallas import tpu as pltpu
from jax.sharding import Mesh, PartitionSpec as P

ITERS = 2
HI = lax.Precision.HIGHEST
B = 128
VMEM_LIMIT = 56 * 1024 * 1024

NT = (((1,), (1,)), ((), ()))
NN = (((1,), (0,)), ((), ()))


def dot(a, b, dims=NN):
    return lax.dot_general(a, b, dims, precision=HI, preferred_element_type=jnp.float32)


def block_pairs(n):
    return [(i, j) for i in range(n) for j in range(i, n)]


def gram_kernel(core_ref, a_ref, out_ref, at_ref):
    n = a_ref.shape[1] // B
    core = core_ref[0]
    at_ref[...] = a_ref[...].T
    pairs = block_pairs(n)
    half = len(pairs) // 2
    place = {pair: index for index, pair in enumerate(pairs)}
    for i in range(n):
        row = dot(at_ref[i * B:(i + 1) * B, :], a_ref[:, i * B:])
        for j in range(i, n):
            index = place[(i, j)]
            slot = core if index < half else 1 - core
            start = (index % half) * B
            out_ref[slot, start:start + B, :] = row[:, (j - i) * B:(j - i + 1) * B]


def local_gram(core, a):
    n = a.shape[1] // B
    half = n * (n + 1) // 4
    return pl.pallas_call(
        gram_kernel,
        out_shape=jax.ShapeDtypeStruct((2, half * B, B), jnp.float32),
        in_specs=[
            pl.BlockSpec(memory_space=pltpu.SMEM),
            pl.BlockSpec(memory_space=pltpu.VMEM),
        ],
        out_specs=pl.BlockSpec(memory_space=pltpu.VMEM),
        scratch_shapes=[pltpu.VMEM((a.shape[1], a.shape[0]), jnp.float32)],
        compiler_params=pltpu.CompilerParams(vmem_limit_bytes=VMEM_LIMIT),
        name="local_gram",
    )(core, a)


def inverse_factor(gram):
    k = gram.shape[0]
    rows = k // 8
    wide = jnp.concatenate([gram, jnp.zeros((k, B - k), jnp.float32)], axis=1)
    tiles = [wide[8 * t:8 * t + 8, :] for t in range(rows)]
    lane = lax.broadcasted_iota(jnp.int32, (8, B), 1)
    sub = lax.broadcasted_iota(jnp.int32, (8, B), 0)
    scale = []
    for j in range(k):
        t, s = divmod(j, 8)
        row = tiles[t][s:s + 1, :]
        pivot = row[:, j:j + 1]
        row = jnp.where(lane[0:1, :] == j, 1.0, row) * (1.0 / pivot)
        scale.append(lax.rsqrt(pivot))
        for u in range(t, rows):
            column = jnp.broadcast_to(tiles[u][:, j:j + 1], (8, B))
            rest = jnp.where(lane == j, 0.0, tiles[u])
            new = rest - column * row
            tiles[u] = jnp.where(sub > s, new, tiles[u]) if u == t else new
    out = []
    for t in range(rows):
        below = jnp.where(lane < sub + 8 * t, tiles[t], 0.0)
        below = jnp.where(lane == sub + 8 * t, 1.0, below)
        out.append(below * jnp.concatenate(scale[8 * t:8 * t + 8], axis=0))
    return jnp.concatenate(out, axis=0)[:, :k]


def iterate_kernel(total, core_ref, own_ref, other_ref, xt_ref, a_ref, row_ref, proj_ref, c_ref):
    n = c_ref.shape[0] // B
    core = core_ref[0]
    pairs = block_pairs(n)
    half = len(pairs) // 2
    for index, (i, j) in enumerate(pairs):
        start = (index % half) * B
        own, other = own_ref[start:start + B, :], other_ref[start:start + B, :]
        mine = (core == 0) if index < half else (core == 1)
        block = jnp.where(mine, own, other)
        c_ref[i * B:(i + 1) * B, j * B:(j + 1) * B] = block
        if i < j:
            c_ref[j * B:(j + 1) * B, i * B:(i + 1) * B] = block.T
    root = math.sqrt(total)
    xt = xt_ref[...]
    for step in range(ITERS + 1):
        zt = dot(xt, c_ref[...])
        inv = inverse_factor(dot(xt, zt, NT))
        crosst = dot(inv, zt)
        if step < ITERS:
            xt = dot(inverse_factor(dot(crosst, crosst, NT)), crosst)
    proj_ref[...] = crosst / root
    y = dot(a_ref[...], xt, NT)
    row_ref[...] = dot(y, inv, NT) * root


def iterate(total, core, own, other, xt, a):
    k, d = xt.shape
    vmem = pl.BlockSpec(memory_space=pltpu.VMEM)
    return pl.pallas_call(
        functools.partial(iterate_kernel, total),
        out_shape=(
            jax.ShapeDtypeStruct((a.shape[0], k), jnp.float32),
            jax.ShapeDtypeStruct((k, d), jnp.float32),
        ),
        in_specs=[pl.BlockSpec(memory_space=pltpu.SMEM)] + [vmem] * 4,
        out_specs=(vmem, vmem),
        scratch_shapes=[pltpu.VMEM((d, d), jnp.float32)],
        compiler_params=pltpu.CompilerParams(vmem_limit_bytes=VMEM_LIMIT),
        name="iterate",
    )(core, own, other, xt, a)


def scatter_sum(v, axes):
    return jnp.sum(lax.all_to_all(v, axes, 0, 0, tiled=True), axis=0)


def collect(v, axes):
    copies = jnp.broadcast_to(v[None], (lax.axis_size(axes),) + v.shape)
    return lax.all_to_all(copies, axes, 0, 0, tiled=True)


def all_sum(v):
    cut = 40 * 32
    first = scatter_sum(v[:cut].reshape(32, -1, B), ("z", "x"))
    second = scatter_sum(v[cut:].reshape(32, -1, B), ("y", "x"))
    first = jnp.sum(collect(first, "y"), axis=0)
    second = jnp.sum(collect(second, "z"), axis=0)
    first = collect(first, ("z", "x"))
    second = collect(second, ("y", "x"))
    return jnp.concatenate([first.reshape(-1, B), second.reshape(-1, B)], axis=0)


def swap(v):
    return lax.ppermute(v, "core", [(0, 1), (1, 0)])


def local(total, slab, test_matrix):
    core = lax.axis_index("core").astype(jnp.int32)[None]
    parts = local_gram(core, slab)
    own = all_sum(parts[0] + swap(parts[1]))
    other = swap(own)
    return iterate(total, core, own, other, test_matrix.T, slab)


def solution(mesh):
    fine = Mesh(mesh.devices.reshape(8, 8, 2, 4), ("y", "z", "core", "x"))
    split = P(("y", "z", "core", "x"), None)

    def run(slab, test_matrix):
        return jax.shard_map(
            functools.partial(local, slab.shape[0]),
            mesh=fine,
            in_specs=(split, P()),
            out_specs=(split, P()),
            check_vma=False,
        )(slab, test_matrix)

    return run
```

```python
import functools
import math

import jax
import jax.numpy as jnp
from jax import lax
from jax.experimental import pallas as pl
from jax.experimental.pallas import tpu as pltpu
from jax.sharding import Mesh, PartitionSpec as P

ITERS = 2
B = 128
T = 256
AXES = ("y", "y_pair", "z", "z_pair", "core", "x")
NEAR = ("y_pair", "z_pair", "x")
FAR = ("z",), ("y",)

NT = (((1,), (1,)), ((), ()))
NN = (((1,), (0,)), ((), ()))

TILES = ((0, 3), (1, 2))
HALVES = tuple(
    tuple((i, j) for tile in tiles for j in (2 * tile, 2 * tile + 1) for i in range(j + 1))
    for tiles in TILES
)


def dot(a, b, dims=NN):
    return lax.dot_general(
        a, b, dims, precision=lax.Precision.HIGHEST, preferred_element_type=jnp.float32
    )


def part_dot(a, b):
    return lax.dot_general(a, b, NN, preferred_element_type=jnp.float32)


def split(x):
    high = x.astype(jnp.bfloat16)
    rest = x - high.astype(jnp.float32)
    mid = rest.astype(jnp.bfloat16)
    low = (rest - mid.astype(jnp.float32)).astype(jnp.bfloat16)
    return high, mid, low


def gram_kernel(half_ref, a_ref, out_ref):
    a = a_ref[...]
    rows = split(a.T)
    columns = split(a)

    def fill(half):
        for tile in TILES[half]:
            size = T * (tile + 1)
            high, mid, low = [part[:, T * tile:size] for part in columns]
            left = [part[:size, :] for part in rows]
            gram = part_dot(left[2], high) + part_dot(left[1], mid) + part_dot(left[0], low)
            gram = gram + (part_dot(left[1], high) + part_dot(left[0], mid))
            gram = gram + part_dot(left[0], high)
            for index, (i, j) in enumerate(HALVES[half]):
                if j // 2 == tile:
                    out_ref[index * B:(index + 1) * B, :] = gram[
                        i * B:(i + 1) * B, (j % 2) * B:(j % 2 + 1) * B
                    ]

    for half in range(2):
        pl.when(half_ref[0] == half)(functools.partial(fill, half))


def gram_half(half, a):
    return pl.pallas_call(
        gram_kernel,
        out_shape=jax.ShapeDtypeStruct((len(HALVES[0]) * B, B), jnp.float32),
        in_specs=[
            pl.BlockSpec(memory_space=pltpu.SMEM),
            pl.BlockSpec(memory_space=pltpu.VMEM),
        ],
        out_specs=pl.BlockSpec(memory_space=pltpu.VMEM),
        compiler_params=pltpu.CompilerParams(vmem_limit_bytes=24 * 1024 * 1024),
        cost_estimate=pl.CostEstimate(
            flops=6 * 2 * 256 * 1280 * 256, bytes_accessed=2300000, transcendentals=0
        ),
        name="gram_half",
    )(half, a)


def inverse_factor(gram, width=4):
    k = gram.shape[0]
    rows = k // 8
    wide = jnp.concatenate([gram, jnp.zeros((k, B - k), jnp.float32)], axis=1)
    tiles = [wide[8 * t:8 * t + 8, :] for t in range(rows)]
    lane = lax.broadcasted_iota(jnp.int32, (8, B), 1)
    sub = lax.broadcasted_iota(jnp.int32, (8, B), 0)

    def row_of(tile, s):
        return jnp.broadcast_to(tile[s:s + 1, :], (8, B))

    def columns(start, first):
        return [
            {u: jnp.broadcast_to(tiles[u][:, c:c + 1], (8, B)) for u in range(first, rows)}
            for c in range(start, min(start + width, k))
        ]

    scale = [None] * rows
    now = columns(0, 0)
    for start in range(0, k, width):
        t = start // 8
        ahead = columns(start + width, t)
        inside = (lane >= start) & (lane < start + width)
        for u in range(t, rows):
            if u == t:
                unit = jnp.where(lane == sub + 8 * u, 1.0, 0.0)
                tiles[u] = jnp.where(inside & (sub >= start % 8), unit, tiles[u])
            else:
                tiles[u] = jnp.where(inside, 0.0, tiles[u])
        for c in range(len(now)):
            s = start % 8 + c
            pivot = row_of(now[c][t], s)
            inverse = 1.0 / pivot
            root = lax.rsqrt(pivot)
            scale[t] = root if s == 0 else jnp.where(sub == s, root, scale[t])
            for other in now[c + 1:] + ahead:
                ratio = row_of(other[t], s) * inverse
                for u in range(t, rows):
                    other[u] = other[u] - now[c][u] * ratio
            row = row_of(tiles[t], s) * inverse
            for u in range(t, rows):
                column = jnp.where(sub > s, now[c][u], 0.0) if u == t else now[c][u]
                tiles[u] = tiles[u] - column * row
        now = ahead
    out = [jnp.where(lane <= sub + 8 * t, tiles[t], 0.0) * scale[t] for t in range(rows)]
    return jnp.concatenate(out, axis=0)[:, :k]


def times_gram(xt, parts):
    k, d = xt.shape
    p = -(-k // 16) * 16
    padded = jnp.concatenate([xt, jnp.zeros((p - k, d), jnp.float32)], axis=0)
    stack = jnp.concatenate(split(padded), axis=0)
    high = part_dot(stack, parts[0][...])
    mid = part_dot(stack[:2 * p], parts[1][...])
    low = part_dot(stack[:p], parts[2][...])
    out = (low + mid[p:] + high[2 * p:]) + (mid[:p] + high[p:2 * p]) + high[:p]
    return out[:k]


def iterate_kernel(total, core_ref, own_ref, other_ref, xt_ref, a_ref, rowt_ref, proj_ref, *parts):
    first = core_ref[0] == 0
    for half in range(2):
        for index, (i, j) in enumerate(HALVES[half]):
            where = slice(index * B, (index + 1) * B)
            mine = first if half == 0 else jnp.logical_not(first)
            block = jnp.where(mine, own_ref[where, :], other_ref[where, :])
            for part, value in zip(parts, split(block)):
                part[i * B:(i + 1) * B, j * B:(j + 1) * B] = value
            if i < j:
                for part, value in zip(parts, split(block.T)):
                    part[j * B:(j + 1) * B, i * B:(i + 1) * B] = value
    root = math.sqrt(total)
    xt = xt_ref[...]
    for step in range(ITERS + 1):
        zt = times_gram(xt, parts)
        inv = inverse_factor(dot(xt, zt, NT))
        crosst = dot(inv, zt)
        if step < ITERS:
            xt = dot(inverse_factor(dot(crosst, crosst, NT)), crosst)
    proj_ref[...] = crosst / root
    rowt_ref[...] = dot(inv, dot(xt, a_ref[...], NT)) * root


def iterate(total, core, own, other, xt, a):
    k, d = xt.shape
    vmem = pl.BlockSpec(memory_space=pltpu.VMEM)
    return pl.pallas_call(
        functools.partial(iterate_kernel, total),
        out_shape=(
            jax.ShapeDtypeStruct((k, a.shape[0]), jnp.float32),
            jax.ShapeDtypeStruct((k, d), jnp.float32),
        ),
        in_specs=[pl.BlockSpec(memory_space=pltpu.SMEM)] + [vmem] * 4,
        out_specs=(vmem, vmem),
        scratch_shapes=[pltpu.VMEM((d, d), jnp.bfloat16)] * 3,
        compiler_params=pltpu.CompilerParams(vmem_limit_bytes=32 * 1024 * 1024),
        name="iterate",
    )(core, own, other, xt, a)


def scatter_sum(v, axes):
    v = v.reshape(lax.axis_size(axes), -1, B)
    return jnp.sum(lax.all_to_all(v, axes, 0, 0, tiled=True), axis=0)


def collect(v, axes):
    copies = jnp.broadcast_to(v[None], (lax.axis_size(axes),) + v.shape)
    return lax.all_to_all(copies, axes, 0, 0, tiled=True)


def all_sum(v):
    v = scatter_sum(v, NEAR)
    for axes in FAR:
        v = jnp.sum(collect(v, axes), axis=0)
    return collect(v, NEAR).reshape(-1, B)


def swap(v):
    return lax.ppermute(v, "core", [(0, 1), (1, 0)])


def local(total, slab, test_matrix):
    core = lax.axis_index("core").astype(jnp.int32)[None]
    there = swap(gram_half(1 - core, slab))
    own = all_sum(gram_half(core, slab) + there)
    rowt, projected = iterate(total, core, own, swap(own), test_matrix.T, slab)
    return rowt.T, projected


def solution(mesh):
    fine = Mesh(mesh.devices.reshape(4, 2, 4, 2, 2, 4), AXES)
    rows = P(AXES, None)

    def run(slab, test_matrix):
        return jax.shard_map(
            functools.partial(local, slab.shape[0]),
            mesh=fine,
            in_specs=(rows, P()),
            out_specs=(rows, P()),
            check_vma=False,
        )(slab, test_matrix)

    return run
```

```python
import functools
import math

import jax
import jax.numpy as jnp
from jax import lax
from jax.experimental import pallas as pl
from jax.experimental.pallas import tpu as pltpu
from jax.sharding import Mesh, PartitionSpec as P

ITERS = 2
B = 128
T = 256
AXES = ("y", "y_pair", "z", "z_pair", "core", "x")
NEAR = ("y_pair", "z_pair", "x")
FAR = ("z",), ("y",)

NT = (((1,), (1,)), ((), ()))
NN = (((1,), (0,)), ((), ()))

TILES = ((0, 3), (1, 2))
PAIRS = tuple(
    tuple((i, j) for tile in tiles for j in (2 * tile, 2 * tile + 1) for i in range(j + 1))
    for tiles in TILES
)
ABOVE = tuple(tuple(pair for pair in pairs if pair[0] < pair[1]) for pairs in PAIRS)
DIAGONAL = tuple(tuple(pair for pair in pairs if pair[0] == pair[1]) for pairs in PAIRS)
PACKED = len(ABOVE[0]) + len(DIAGONAL[0]) - 1
H = B // 2


def dot(a, b, dims=NN):
    return lax.dot_general(
        a, b, dims, precision=lax.Precision.HIGHEST, preferred_element_type=jnp.float32
    )


def part_dot(a, b):
    return lax.dot_general(a, b, NN, preferred_element_type=jnp.float32)


def split(x):
    high = x.astype(jnp.bfloat16)
    rest = x - high.astype(jnp.float32)
    mid = rest.astype(jnp.bfloat16)
    low = (rest - mid.astype(jnp.float32)).astype(jnp.bfloat16)
    return high, mid, low


def block_of(ref, index):
    return ref[index * B:(index + 1) * B, :]


def gram_kernel(half_ref, a_ref, *refs):
    before, out_ref = refs if len(refs) == 2 else (None, refs[0])
    a = a_ref[...]
    rows = split(a.T)
    columns = split(a)
    left_lanes = lax.broadcasted_iota(jnp.int32, (H, B), 1) < H

    def put(index, value):
        if before is not None:
            value = value + block_of(before, index)
        out_ref[index * B:(index + 1) * B, :] = value

    def fill(half):
        diagonal = []
        for tile in TILES[half]:
            size = T * (tile + 1)
            high, mid, low = [part[:, T * tile:size] for part in columns]
            left = [part[:size, :] for part in rows]
            gram = part_dot(left[2], high) + part_dot(left[1], mid) + part_dot(left[0], low)
            gram = gram + (part_dot(left[1], high) + part_dot(left[0], mid))
            gram = gram + part_dot(left[0], high)
            for i, j in PAIRS[half]:
                if j // 2 == tile:
                    block = gram[i * B:(i + 1) * B, (j % 2) * B:(j % 2 + 1) * B]
                    if i == j:
                        diagonal.append(block)
                    else:
                        put(ABOVE[half].index((i, j)), block)
        last = diagonal.pop()
        guests = (last[:H], pltpu.roll(last[:H], H, 1), pltpu.roll(last[H:], H, 1))
        for index, (block, guest) in enumerate(zip(diagonal, guests)):
            lower = jnp.where(left_lanes, guest, block[H:])
            put(len(ABOVE[half]) + index, jnp.concatenate([block[:H], lower], axis=0))

    for half in range(2):
        pl.when(half_ref[0] == half)(functools.partial(fill, half))


def gram_half(half, a, *before):
    vmem = pl.BlockSpec(memory_space=pltpu.VMEM)
    return pl.pallas_call(
        gram_kernel,
        out_shape=jax.ShapeDtypeStruct((PACKED * B, B), jnp.float32),
        in_specs=[pl.BlockSpec(memory_space=pltpu.SMEM), vmem] + [vmem] * len(before),
        out_specs=vmem,
        compiler_params=pltpu.CompilerParams(vmem_limit_bytes=24 * 1024 * 1024),
        cost_estimate=pl.CostEstimate(
            flops=6 * 2 * 256 * 1280 * 256, bytes_accessed=2300000, transcendentals=0
        ),
        name="gram_half",
    )(half, a, *before)


def unpack(half, blocks):
    count = len(ABOVE[half])
    low_rows = lax.broadcasted_iota(jnp.int32, (B, B), 0) >= H
    left = lax.broadcasted_iota(jnp.int32, (B, B), 1) < H
    guests = [block[H:] for block in blocks[count:]]
    upper = jnp.where(left[:H], guests[0], pltpu.roll(guests[1], H, 1))
    last = jnp.concatenate([upper, pltpu.roll(guests[2], H, 1)], axis=0)
    for pair, block in zip(ABOVE[half], blocks):
        yield pair, block
    for pair, block in zip(DIAGONAL[half], list(blocks[count:]) + [last]):
        yield pair, jnp.where(low_rows & left, block.T, block)


def inverse_factor(gram, width=4):
    k = gram.shape[0]
    rows = k // 8
    wide = jnp.concatenate([gram, jnp.zeros((k, B - k), jnp.float32)], axis=1)
    tiles = [wide[8 * t:8 * t + 8, :] for t in range(rows)]
    lane = lax.broadcasted_iota(jnp.int32, (8, B), 1)
    sub = lax.broadcasted_iota(jnp.int32, (8, B), 0)

    def row_of(tile, s):
        return jnp.broadcast_to(tile[s:s + 1, :], (8, B))

    def columns(start, first):
        return [
            {u: jnp.broadcast_to(tiles[u][:, c:c + 1], (8, B)) for u in range(first, rows)}
            for c in range(start, min(start + width, k))
        ]

    scale = [None] * rows
    now = columns(0, 0)
    for start in range(0, k, width):
        t, top = divmod(start, 8)
        ahead = columns(start + width, t)
        inside = (lane >= start) & (lane < start + width)
        unit = jnp.where(lane == sub + 8 * t, 1.0, 0.0)
        tiles[t] = jnp.where(inside & (sub >= top), unit, tiles[t])
        n = len(now)
        own = {(a, b): row_of(now[b][t], top + a) for a in range(n) for b in range(a + 1)}
        inverse, lower = [], {}
        for c in range(n):
            inverse.append(1.0 / own[c, c])
            root = lax.rsqrt(own[c, c])
            scale[t] = root if top + c == 0 else jnp.where(sub == top + c, root, scale[t])
            for a in range(c + 1, n):
                lower[a, c] = own[a, c] * inverse[c]
                for b in range(c + 1, a + 1):
                    own[a, b] = own[a, b] - lower[a, c] * own[b, c]
        ratios, lines = [], []
        for c in range(n):
            for o in range(c + 1, n):
                now[o][t] = now[o][t] - now[c][t] * lower[o, c]
            ratios.append([row_of(other[t], top + c) * inverse[c] for other in ahead])
            lines.append(row_of(tiles[t], top + c) * inverse[c])
            for other, ratio in zip(ahead, ratios[c]):
                other[t] = other[t] - now[c][t] * ratio
            tiles[t] = tiles[t] - jnp.where(sub > top + c, now[c][t], 0.0) * lines[c]
        for u in range(t + 1, rows):
            tiles[u] = jnp.where(inside, 0.0, tiles[u])
            for c in range(n):
                for o in range(c + 1, n):
                    now[o][u] = now[o][u] - now[c][u] * lower[o, c]
                for other, ratio in zip(ahead, ratios[c]):
                    other[u] = other[u] - now[c][u] * ratio
                tiles[u] = tiles[u] - now[c][u] * lines[c]
        now = ahead
    out = [jnp.where(lane <= sub + 8 * t, tiles[t], 0.0) * scale[t] for t in range(rows)]
    return jnp.concatenate(out, axis=0)[:, :k]


def times_gram(xt, parts):
    k, d = xt.shape
    p = -(-k // 16) * 16
    padded = jnp.concatenate([xt, jnp.zeros((p - k, d), jnp.float32)], axis=0)
    stack = jnp.concatenate(split(padded), axis=0)
    high = part_dot(stack, parts[0][...])
    mid = part_dot(stack[:2 * p], parts[1][...])
    low = part_dot(stack[:p], parts[2][...])
    out = (low + mid[p:] + high[2 * p:]) + (mid[:p] + high[p:2 * p]) + high[:p]
    return out[:k]


def fill_parts(half, packed, parts):
    blocks = [block_of(packed, index) for index in range(PACKED)]
    for (i, j), block in unpack(half, blocks):
        for part, value in zip(parts, split(block)):
            part[i * B:(i + 1) * B, j * B:(j + 1) * B] = value
        if i < j:
            for part, value in zip(parts, split(block.T)):
                part[j * B:(j + 1) * B, i * B:(i + 1) * B] = value


def iterate_kernel(total, core_ref, own_ref, other_ref, xt_ref, a_ref, rowt_ref, proj_ref, *parts):
    first = core_ref[0] == 0
    fill_parts(0, jnp.where(first, own_ref[...], other_ref[...]), parts)
    fill_parts(1, jnp.where(first, other_ref[...], own_ref[...]), parts)
    root = math.sqrt(total)
    xt = xt_ref[...]
    for step in range(ITERS + 1):
        zt = times_gram(xt, parts)
        inv = inverse_factor(dot(xt, zt, NT))
        crosst = dot(inv, zt)
        if step < ITERS:
            xt = dot(inverse_factor(dot(crosst, crosst, NT)), crosst)
    proj_ref[...] = crosst / root
    rowt_ref[...] = dot(inv, dot(xt, a_ref[...], NT)) * root


def iterate(total, core, own, other, xt, a):
    k, d = xt.shape
    vmem = pl.BlockSpec(memory_space=pltpu.VMEM)
    return pl.pallas_call(
        functools.partial(iterate_kernel, total),
        out_shape=(
            jax.ShapeDtypeStruct((k, a.shape[0]), jnp.float32),
            jax.ShapeDtypeStruct((k, d), jnp.float32),
        ),
        in_specs=[pl.BlockSpec(memory_space=pltpu.SMEM)] + [vmem] * 4,
        out_specs=(vmem, vmem),
        scratch_shapes=[pltpu.VMEM((d, d), jnp.bfloat16)] * 3,
        compiler_params=pltpu.CompilerParams(vmem_limit_bytes=32 * 1024 * 1024),
        name="iterate",
    )(core, own, other, xt, a)


def scatter_sum(v, axes):
    v = v.reshape(lax.axis_size(axes), -1, B)
    return jnp.sum(lax.all_to_all(v, axes, 0, 0, tiled=True), axis=0)


def collect(v, axes):
    copies = jnp.broadcast_to(v[None], (lax.axis_size(axes),) + v.shape)
    return lax.all_to_all(copies, axes, 0, 0, tiled=True)


def all_sum(v):
    v = scatter_sum(v, NEAR)
    for axes in FAR:
        v = jnp.sum(collect(v, axes), axis=0)
    return collect(v, NEAR).reshape(-1, B)


def swap(v):
    return lax.ppermute(v, "core", [(0, 1), (1, 0)])


def local(total, slab, test_matrix):
    core = lax.axis_index("core").astype(jnp.int32)[None]
    there = swap(slab)
    own = all_sum(gram_half(core, there, gram_half(core, slab)))
    rowt, projected = iterate(total, core, own, swap(own), test_matrix.T, slab)
    return rowt.T, projected


def solution(mesh):
    fine = Mesh(mesh.devices.reshape(4, 2, 4, 2, 2, 4), AXES)
    rows = P(AXES, None)

    def run(slab, test_matrix):
        return jax.shard_map(
            functools.partial(local, slab.shape[0]),
            mesh=fine,
            in_specs=(rows, P()),
            out_specs=(rows, P()),
            check_vma=False,
        )(slab, test_matrix)

    return run
```

```python
import functools
import math

import jax
import jax.numpy as jnp
from jax import lax
from jax.experimental import pallas as pl
from jax.experimental.pallas import tpu as pltpu
from jax.sharding import Mesh, PartitionSpec as P

ITERS = 2
B = 128
T = 256
AXES = ("y", "y_pair", "z", "z_pair", "core", "x")
NEAR = ("y_pair", "z_pair", "x")
FAR = ("z",), ("y",)

NT = (((1,), (1,)), ((), ()))
NN = (((1,), (0,)), ((), ()))

TILES = ((0, 3), (1, 2))
PAIRS = tuple(
    tuple((i, j) for tile in tiles for j in (2 * tile, 2 * tile + 1) for i in range(j + 1))
    for tiles in TILES
)
ABOVE = tuple(tuple(pair for pair in pairs if pair[0] < pair[1]) for pairs in PAIRS)
DIAGONAL = tuple(tuple(pair for pair in pairs if pair[0] == pair[1]) for pairs in PAIRS)
PACKED = len(ABOVE[0]) + len(DIAGONAL[0]) - 1
H = B // 2


def dot(a, b, dims=NN):
    return lax.dot_general(
        a, b, dims, precision=lax.Precision.HIGHEST, preferred_element_type=jnp.float32
    )


def part_dot(a, b):
    return lax.dot_general(a, b, NN, preferred_element_type=jnp.float32)


def split(x):
    high = x.astype(jnp.bfloat16)
    rest = x - high.astype(jnp.float32)
    mid = rest.astype(jnp.bfloat16)
    low = (rest - mid.astype(jnp.float32)).astype(jnp.bfloat16)
    return high, mid, low


def block_of(ref, index):
    return ref[index * B:(index + 1) * B, :]


def gram_kernel(half_ref, a_ref, *refs):
    before, out_ref = refs if len(refs) == 2 else (None, refs[0])
    left_lanes = lax.broadcasted_iota(jnp.int32, (H, B), 1) < H

    def put(index, value):
        if before is not None:
            value = value + block_of(before, index)
        out_ref[index * B:(index + 1) * B, :] = value

    def fill(half):
        order = []
        for tile in TILES[half]:
            order += [(tile, tile)] + [(other, tile) for other in range(tile)]
        ready, diagonal = {}, {}

        def take(tile):
            if tile not in ready:
                value = a_ref[:, T * tile:T * (tile + 1)]
                ready[tile] = split(value.T), split(value)
            return ready[tile]

        for row, column in order:
            right, left = take(column)[1], take(row)[0]
            gram = part_dot(left[2], right[0]) + part_dot(left[1], right[1])
            gram = gram + part_dot(left[0], right[2])
            gram = gram + (part_dot(left[1], right[0]) + part_dot(left[0], right[1]))
            gram = gram + part_dot(left[0], right[0])
            for r in range(2):
                for c in range(2):
                    pair = (2 * row + r, 2 * column + c)
                    block = gram[r * B:(r + 1) * B, c * B:(c + 1) * B]
                    if pair in DIAGONAL[half]:
                        diagonal[pair] = block
                    elif pair in ABOVE[half]:
                        put(ABOVE[half].index(pair), block)
        *hosts, last = [diagonal[pair] for pair in DIAGONAL[half]]
        guests = (last[:H], pltpu.roll(last[:H], H, 1), pltpu.roll(last[H:], H, 1))
        for index, (block, guest) in enumerate(zip(hosts, guests)):
            lower = jnp.where(left_lanes, guest, block[H:])
            put(len(ABOVE[half]) + index, jnp.concatenate([block[:H], lower], axis=0))

    for half in range(2):
        pl.when(half_ref[0] == half)(functools.partial(fill, half))


def gram_half(half, a, *before):
    vmem = pl.BlockSpec(memory_space=pltpu.VMEM)
    return pl.pallas_call(
        gram_kernel,
        out_shape=jax.ShapeDtypeStruct((PACKED * B, B), jnp.float32),
        in_specs=[pl.BlockSpec(memory_space=pltpu.SMEM), vmem] + [vmem] * len(before),
        out_specs=vmem,
        compiler_params=pltpu.CompilerParams(vmem_limit_bytes=24 * 1024 * 1024),
        cost_estimate=pl.CostEstimate(
            flops=6 * 2 * 256 * 1280 * 256, bytes_accessed=2300000, transcendentals=0
        ),
        name="gram_half",
    )(half, a, *before)


def unpack(half, blocks):
    count = len(ABOVE[half])
    low_rows = lax.broadcasted_iota(jnp.int32, (B, B), 0) >= H
    left = lax.broadcasted_iota(jnp.int32, (B, B), 1) < H
    guests = [block[H:] for block in blocks[count:]]
    upper = jnp.where(left[:H], guests[0], pltpu.roll(guests[1], H, 1))
    last = jnp.concatenate([upper, pltpu.roll(guests[2], H, 1)], axis=0)
    for pair, block in zip(ABOVE[half], blocks):
        yield pair, block
    for pair, block in zip(DIAGONAL[half], list(blocks[count:]) + [last]):
        yield pair, jnp.where(low_rows & left, block.T, block)


def inverse_factor(gram, width=4):
    k = gram.shape[0]
    rows = k // 8
    wide = jnp.concatenate([gram, jnp.zeros((k, B - k), jnp.float32)], axis=1)
    tiles = [wide[8 * t:8 * t + 8, :] for t in range(rows)]
    lane = lax.broadcasted_iota(jnp.int32, (8, B), 1)
    sub = lax.broadcasted_iota(jnp.int32, (8, B), 0)

    def row_of(tile, s):
        return jnp.broadcast_to(tile[s:s + 1, :], (8, B))

    def columns(start, first):
        return [
            {u: jnp.broadcast_to(tiles[u][:, c:c + 1], (8, B)) for u in range(first, rows)}
            for c in range(start, min(start + width, k))
        ]

    scale = [None] * rows
    now = columns(0, 0)
    for start in range(0, k, width):
        t, top = divmod(start, 8)
        ahead = columns(start + width, t)
        inside = (lane >= start) & (lane < start + width)
        unit = jnp.where(lane == sub + 8 * t, 1.0, 0.0)
        tiles[t] = jnp.where(inside & (sub >= top), unit, tiles[t])
        n = len(now)
        own = {(a, b): row_of(now[b][t], top + a) for a in range(n) for b in range(a + 1)}
        inverse, lower = [], {}
        for c in range(n):
            inverse.append(1.0 / own[c, c])
            root = lax.rsqrt(own[c, c])
            scale[t] = root if top + c == 0 else jnp.where(sub == top + c, root, scale[t])
            for a in range(c + 1, n):
                lower[a, c] = own[a, c] * inverse[c]
                for b in range(c + 1, a + 1):
                    own[a, b] = own[a, b] - lower[a, c] * own[b, c]
        ratios, lines = [], []
        for c in range(n):
            for o in range(c + 1, n):
                now[o][t] = now[o][t] - now[c][t] * lower[o, c]
            ratios.append([row_of(other[t], top + c) * inverse[c] for other in ahead])
            lines.append(row_of(tiles[t], top + c) * inverse[c])
            for other, ratio in zip(ahead, ratios[c]):
                other[t] = other[t] - now[c][t] * ratio
            tiles[t] = tiles[t] - jnp.where(sub > top + c, now[c][t], 0.0) * lines[c]
        for u in range(t + 1, rows):
            tiles[u] = jnp.where(inside, 0.0, tiles[u])
            for c in range(n):
                for o in range(c + 1, n):
                    now[o][u] = now[o][u] - now[c][u] * lower[o, c]
                for other, ratio in zip(ahead, ratios[c]):
                    other[u] = other[u] - now[c][u] * ratio
                tiles[u] = tiles[u] - now[c][u] * lines[c]
        now = ahead
    out = [jnp.where(lane <= sub + 8 * t, tiles[t], 0.0) * scale[t] for t in range(rows)]
    return jnp.concatenate(out, axis=0)[:, :k]


def times_gram(xt, parts):
    k, d = xt.shape
    p = -(-k // 16) * 16
    padded = jnp.concatenate([xt, jnp.zeros((p - k, d), jnp.float32)], axis=0)
    stack = jnp.concatenate(split(padded), axis=0)
    high = part_dot(stack, parts[0][...])
    mid = part_dot(stack[:2 * p], parts[1][...])
    low = part_dot(stack[:p], parts[2][...])
    out = (low + mid[p:] + high[2 * p:]) + (mid[:p] + high[p:2 * p]) + high[:p]
    return out[:k]


def fill_parts(half, packed, parts):
    blocks = [block_of(packed, index) for index in range(PACKED)]
    for (i, j), block in unpack(half, blocks):
        for part, value in zip(parts, split(block)):
            part[i * B:(i + 1) * B, j * B:(j + 1) * B] = value
        if i < j:
            for part, value in zip(parts, split(block.T)):
                part[j * B:(j + 1) * B, i * B:(i + 1) * B] = value


def iterate_kernel(total, core_ref, own_ref, other_ref, xt_ref, a_ref, rowt_ref, proj_ref, *parts):
    first = core_ref[0] == 0
    fill_parts(0, jnp.where(first, own_ref[...], other_ref[...]), parts)
    fill_parts(1, jnp.where(first, other_ref[...], own_ref[...]), parts)
    root = math.sqrt(total)
    xt = xt_ref[...]
    for step in range(ITERS + 1):
        zt = times_gram(xt, parts)
        gram = dot(xt, zt, NT)
        if step == ITERS:
            yt = dot(xt, a_ref[...], NT)
        inv = inverse_factor(gram)
        crosst = dot(inv, zt)
        if step < ITERS:
            xt = dot(inverse_factor(dot(crosst, crosst, NT)), crosst)
    proj_ref[...] = crosst / root
    rowt_ref[...] = dot(inv, yt) * root


def iterate(total, core, own, other, xt, a):
    k, d = xt.shape
    vmem = pl.BlockSpec(memory_space=pltpu.VMEM)
    return pl.pallas_call(
        functools.partial(iterate_kernel, total),
        out_shape=(
            jax.ShapeDtypeStruct((k, a.shape[0]), jnp.float32),
            jax.ShapeDtypeStruct((k, d), jnp.float32),
        ),
        in_specs=[pl.BlockSpec(memory_space=pltpu.SMEM)] + [vmem] * 4,
        out_specs=(vmem, vmem),
        scratch_shapes=[pltpu.VMEM((d, d), jnp.bfloat16)] * 3,
        compiler_params=pltpu.CompilerParams(vmem_limit_bytes=32 * 1024 * 1024),
        name="iterate",
    )(core, own, other, xt, a)


def scatter_sum(v, axes):
    v = v.reshape(lax.axis_size(axes), -1, B)
    return jnp.sum(lax.all_to_all(v, axes, 0, 0, tiled=True), axis=0)


def collect(v, axes):
    copies = jnp.broadcast_to(v[None], (lax.axis_size(axes),) + v.shape)
    return lax.all_to_all(copies, axes, 0, 0, tiled=True)


def all_sum(v):
    v = scatter_sum(v, NEAR)
    for axes in FAR:
        v = jnp.sum(collect(v, axes), axis=0)
    return collect(v, NEAR).reshape(-1, B)


def swap(v):
    return lax.ppermute(v, "core", [(0, 1), (1, 0)])


def local(total, slab, test_matrix):
    core = lax.axis_index("core").astype(jnp.int32)[None]
    there = swap(slab)
    own = all_sum(gram_half(core, there, gram_half(core, slab)))
    rowt, projected = iterate(total, core, own, swap(own), test_matrix.T, slab)
    return rowt.T, projected


def solution(mesh):
    fine = Mesh(mesh.devices.reshape(4, 2, 4, 2, 2, 4), AXES)
    rows = P(AXES, None)

    def run(slab, test_matrix):
        return jax.shard_map(
            functools.partial(local, slab.shape[0]),
            mesh=fine,
            in_specs=(rows, P()),
            out_specs=(rows, P()),
            check_vma=False,
        )(slab, test_matrix)

    return run
```

```python
import functools
import math

import jax
import jax.numpy as jnp
from jax import lax
from jax.experimental import pallas as pl
from jax.experimental.pallas import tpu as pltpu
from jax.sharding import Mesh, PartitionSpec as P

ITERS = 2
B = 128
T = 256
X, Y, Z = 4, 8, 8


def device(y, z, core, x):
    return ((y % Y * Z + z % Z) * 2 + core) * X + x % X


NEAR = [
    [device(y + core + a, z + core + b, core, x + core + c)
     for a in range(2) for b in range(2) for c in range(2)]
    for core in range(2) for y in range(0, Y, 2) for z in range(0, Z, 2) for x in range(0, X, 2)
]
FAR = [
    [device(y + a, z + b, core, x + c)
     for y in range(0, Y, 2) for z in range(0, Z, 2) for x in range(0, X, 2)]
    for core in range(2) for a in range(2) for b in range(2) for c in range(2)
]
SWAP = [
    (device(y, z, core, x), device(y, z, 1 - core, x))
    for y in range(Y) for z in range(Z) for core in range(2) for x in range(X)
]

NT = (((1,), (1,)), ((), ()))
NN = (((1,), (0,)), ((), ()))

TILES = ((0, 3), (1, 2))
PAIRS = tuple(
    tuple((i, j) for tile in tiles for j in (2 * tile, 2 * tile + 1) for i in range(j + 1))
    for tiles in TILES
)
ABOVE = tuple(tuple(pair for pair in pairs if pair[0] < pair[1]) for pairs in PAIRS)
DIAGONAL = tuple(tuple(pair for pair in pairs if pair[0] == pair[1]) for pairs in PAIRS)
PACKED = len(ABOVE[0]) + len(DIAGONAL[0]) - 1
H = B // 2


def dot(a, b, dims=NN):
    return lax.dot_general(
        a, b, dims, precision=lax.Precision.HIGHEST, preferred_element_type=jnp.float32
    )


def part_dot(a, b):
    return lax.dot_general(a, b, NN, preferred_element_type=jnp.float32)


def split(x):
    high = x.astype(jnp.bfloat16)
    rest = x - high.astype(jnp.float32)
    mid = rest.astype(jnp.bfloat16)
    low = (rest - mid.astype(jnp.float32)).astype(jnp.bfloat16)
    return high, mid, low


def block_of(ref, index):
    return ref[index * B:(index + 1) * B, :]


def gram_kernel(half_ref, a_ref, *refs):
    before, out_ref = refs if len(refs) == 2 else (None, refs[0])
    left_lanes = lax.broadcasted_iota(jnp.int32, (H, B), 1) < H

    def put(index, value):
        if before is not None:
            value = value + block_of(before, index)
        out_ref[index * B:(index + 1) * B, :] = value

    def fill(half):
        order = []
        for tile in TILES[half]:
            order += [(tile, tile)] + [(other, tile) for other in range(tile)]
        ready, diagonal = {}, {}

        def take(tile):
            if tile not in ready:
                value = a_ref[:, T * tile:T * (tile + 1)]
                ready[tile] = split(value.T), split(value)
            return ready[tile]

        for row, column in order:
            right, left = take(column)[1], take(row)[0]
            gram = part_dot(left[2], right[0]) + part_dot(left[1], right[1])
            gram = gram + part_dot(left[0], right[2])
            gram = gram + (part_dot(left[1], right[0]) + part_dot(left[0], right[1]))
            gram = gram + part_dot(left[0], right[0])
            for r in range(2):
                for c in range(2):
                    pair = (2 * row + r, 2 * column + c)
                    block = gram[r * B:(r + 1) * B, c * B:(c + 1) * B]
                    if pair in DIAGONAL[half]:
                        diagonal[pair] = block
                    elif pair in ABOVE[half]:
                        put(ABOVE[half].index(pair), block)
        *hosts, last = [diagonal[pair] for pair in DIAGONAL[half]]
        guests = (last[:H], pltpu.roll(last[:H], H, 1), pltpu.roll(last[H:], H, 1))
        for index, (block, guest) in enumerate(zip(hosts, guests)):
            lower = jnp.where(left_lanes, guest, block[H:])
            put(len(ABOVE[half]) + index, jnp.concatenate([block[:H], lower], axis=0))

    for half in range(2):
        pl.when(half_ref[0] == half)(functools.partial(fill, half))


def gram_half(half, a, *before):
    vmem = pl.BlockSpec(memory_space=pltpu.VMEM)
    return pl.pallas_call(
        gram_kernel,
        out_shape=jax.ShapeDtypeStruct((PACKED * B, B), jnp.float32),
        in_specs=[pl.BlockSpec(memory_space=pltpu.SMEM), vmem] + [vmem] * len(before),
        out_specs=vmem,
        compiler_params=pltpu.CompilerParams(vmem_limit_bytes=24 * 1024 * 1024),
        cost_estimate=pl.CostEstimate(
            flops=6 * 2 * 256 * 1280 * 256, bytes_accessed=2300000, transcendentals=0
        ),
        name="gram_half",
    )(half, a, *before)


def unpack(half, blocks):
    count = len(ABOVE[half])
    low_rows = lax.broadcasted_iota(jnp.int32, (B, B), 0) >= H
    left = lax.broadcasted_iota(jnp.int32, (B, B), 1) < H
    guests = [block[H:] for block in blocks[count:]]
    upper = jnp.where(left[:H], guests[0], pltpu.roll(guests[1], H, 1))
    last = jnp.concatenate([upper, pltpu.roll(guests[2], H, 1)], axis=0)
    for pair, block in zip(ABOVE[half], blocks):
        yield pair, block
    for pair, block in zip(DIAGONAL[half], list(blocks[count:]) + [last]):
        yield pair, jnp.where(low_rows & left, block.T, block)


def inverse_factor(gram, width=4):
    k = gram.shape[0]
    rows = k // 8
    wide = jnp.concatenate([gram, jnp.zeros((k, B - k), jnp.float32)], axis=1)
    tiles = [wide[8 * t:8 * t + 8, :] for t in range(rows)]
    lane = lax.broadcasted_iota(jnp.int32, (8, B), 1)
    sub = lax.broadcasted_iota(jnp.int32, (8, B), 0)

    def row_of(tile, s):
        return jnp.broadcast_to(tile[s:s + 1, :], (8, B))

    def columns(start, first):
        return [
            {u: jnp.broadcast_to(tiles[u][:, c:c + 1], (8, B)) for u in range(first, rows)}
            for c in range(start, min(start + width, k))
        ]

    scale = [None] * rows
    now = columns(0, 0)
    for start in range(0, k, width):
        t, top = divmod(start, 8)
        ahead = columns(start + width, t)
        inside = (lane >= start) & (lane < start + width)
        unit = jnp.where(lane == sub + 8 * t, 1.0, 0.0)
        tiles[t] = jnp.where(inside & (sub >= top), unit, tiles[t])
        n = len(now)
        own = {(a, b): row_of(now[b][t], top + a) for a in range(n) for b in range(a + 1)}
        inverse, lower = [], {}
        for c in range(n):
            inverse.append(1.0 / own[c, c])
            root = lax.rsqrt(own[c, c])
            scale[t] = root if top + c == 0 else jnp.where(sub == top + c, root, scale[t])
            for a in range(c + 1, n):
                lower[a, c] = own[a, c] * inverse[c]
                for b in range(c + 1, a + 1):
                    own[a, b] = own[a, b] - lower[a, c] * own[b, c]
        ratios, lines = [], []
        for c in range(n):
            for o in range(c + 1, n):
                now[o][t] = now[o][t] - now[c][t] * lower[o, c]
            ratios.append([row_of(other[t], top + c) * inverse[c] for other in ahead])
            lines.append(row_of(tiles[t], top + c) * inverse[c])
            for other, ratio in zip(ahead, ratios[c]):
                other[t] = other[t] - now[c][t] * ratio
            tiles[t] = tiles[t] - jnp.where(sub > top + c, now[c][t], 0.0) * lines[c]
        for u in range(t + 1, rows):
            tiles[u] = jnp.where(inside, 0.0, tiles[u])
            for c in range(n):
                for o in range(c + 1, n):
                    now[o][u] = now[o][u] - now[c][u] * lower[o, c]
                for other, ratio in zip(ahead, ratios[c]):
                    other[u] = other[u] - now[c][u] * ratio
                tiles[u] = tiles[u] - now[c][u] * lines[c]
        now = ahead
    out = [jnp.where(lane <= sub + 8 * t, tiles[t], 0.0) * scale[t] for t in range(rows)]
    return jnp.concatenate(out, axis=0)[:, :k]


def times_gram(xt, parts):
    k, d = xt.shape
    p = -(-k // 16) * 16
    padded = jnp.concatenate([xt, jnp.zeros((p - k, d), jnp.float32)], axis=0)
    stack = jnp.concatenate(split(padded), axis=0)
    high = part_dot(stack, parts[0][...])
    mid = part_dot(stack[:2 * p], parts[1][...])
    low = part_dot(stack[:p], parts[2][...])
    out = (low + mid[p:] + high[2 * p:]) + (mid[:p] + high[p:2 * p]) + high[:p]
    return out[:k]


def fill_parts(half, packed, parts):
    blocks = [block_of(packed, index) for index in range(PACKED)]
    for (i, j), block in unpack(half, blocks):
        for part, value in zip(parts, split(block)):
            part[i * B:(i + 1) * B, j * B:(j + 1) * B] = value
        if i < j:
            for part, value in zip(parts, split(block.T)):
                part[j * B:(j + 1) * B, i * B:(i + 1) * B] = value


def iterate_kernel(total, core_ref, own_ref, other_ref, xt_ref, a_ref, rowt_ref, proj_ref, *parts):
    first = core_ref[0] == 0
    fill_parts(0, jnp.where(first, own_ref[...], other_ref[...]), parts)
    fill_parts(1, jnp.where(first, other_ref[...], own_ref[...]), parts)
    root = math.sqrt(total)
    xt = xt_ref[...]
    for step in range(ITERS + 1):
        zt = times_gram(xt, parts)
        gram = dot(xt, zt, NT)
        if step == ITERS:
            yt = dot(xt, a_ref[...], NT)
        inv = inverse_factor(gram)
        crosst = dot(inv, zt)
        if step < ITERS:
            xt = dot(inverse_factor(dot(crosst, crosst, NT)), crosst)
    proj_ref[...] = crosst / root
    rowt_ref[...] = dot(inv, yt) * root


def iterate(total, core, own, other, xt, a):
    k, d = xt.shape
    vmem = pl.BlockSpec(memory_space=pltpu.VMEM)
    return pl.pallas_call(
        functools.partial(iterate_kernel, total),
        out_shape=(
            jax.ShapeDtypeStruct((k, a.shape[0]), jnp.float32),
            jax.ShapeDtypeStruct((k, d), jnp.float32),
        ),
        in_specs=[pl.BlockSpec(memory_space=pltpu.SMEM)] + [vmem] * 4,
        out_specs=(vmem, vmem),
        scratch_shapes=[pltpu.VMEM((d, d), jnp.bfloat16)] * 3,
        compiler_params=pltpu.CompilerParams(vmem_limit_bytes=32 * 1024 * 1024),
        name="iterate",
    )(core, own, other, xt, a)


def exchange(v, groups):
    return lax.all_to_all(v, "device", 0, 0, axis_index_groups=groups, tiled=True)


def scatter_sum(v, groups):
    return jnp.sum(exchange(v.reshape(len(groups[0]), -1, B), groups), axis=0)


def collect(v, groups):
    copies = jnp.broadcast_to(v[None], (len(groups[0]),) + v.shape)
    return exchange(copies, groups).reshape(-1, B)


def all_sum(v):
    v = scatter_sum(v, NEAR)
    rows = v.shape[0]
    v = jnp.pad(v, ((0, -rows % len(FAR[0])), (0, 0)))
    v = collect(scatter_sum(v, FAR), FAR)[:rows]
    return collect(v, NEAR)


def swap(v):
    return lax.ppermute(v, "device", SWAP)


def local(total, slab, test_matrix):
    core = (lax.axis_index("device") // X % 2).astype(jnp.int32)[None]
    there = swap(slab)
    own = all_sum(gram_half(core, there, gram_half(core, slab)))
    rowt, projected = iterate(total, core, own, swap(own), test_matrix.T, slab)
    return rowt.T, projected


def solution(mesh):
    flat = Mesh(mesh.devices.reshape(-1), ("device",))
    rows = P("device", None)

    def run(slab, test_matrix):
        return jax.shard_map(
            functools.partial(local, slab.shape[0]),
            mesh=flat,
            in_specs=(rows, P()),
            out_specs=(rows, P()),
            check_vma=False,
        )(slab, test_matrix)

    return run
```

```python
import functools
import math

import jax
import jax.numpy as jnp
from jax import lax
from jax.experimental import pallas as pl
from jax.experimental.pallas import tpu as pltpu
from jax.sharding import Mesh, PartitionSpec as P

ITERS = 2
B = 128
T = 256
X, Y, Z = 4, 8, 8


def device(y, z, core, x):
    return ((y % Y * Z + z % Z) * 2 + core) * X + x % X


NEAR = [
    [device(y + core + a, z + core + b, core, x)
     for a in range(2) for b in range(2) for x in range(X)]
    for core in range(2) for y in range(0, Y, 2) for z in range(0, Z, 2)
]
FAR = (
    [
        [device(y, z + a, core, x) for z in range(0, Z, 2)]
        for y in range(Y) for core in range(2) for x in range(X) for a in range(2)
    ],
    [
        [device(y + a, z, core, x) for y in range(0, Y, 2)]
        for z in range(Z) for core in range(2) for x in range(X) for a in range(2)
    ],
)
SWAP = [
    (device(y, z, core, x), device(y, z, 1 - core, x))
    for y in range(Y) for z in range(Z) for core in range(2) for x in range(X)
]

NT = (((1,), (1,)), ((), ()))
NN = (((1,), (0,)), ((), ()))

TILES = ((0, 3), (1, 2))
PAIRS = tuple(
    tuple((i, j) for tile in tiles for j in (2 * tile, 2 * tile + 1) for i in range(j + 1))
    for tiles in TILES
)
ABOVE = tuple(tuple(pair for pair in pairs if pair[0] < pair[1]) for pairs in PAIRS)
DIAGONAL = tuple(tuple(pair for pair in pairs if pair[0] == pair[1]) for pairs in PAIRS)
PACKED = len(ABOVE[0]) + len(DIAGONAL[0]) - 1
H = B // 2


def dot(a, b, dims=NN):
    return lax.dot_general(
        a, b, dims, precision=lax.Precision.HIGHEST, preferred_element_type=jnp.float32
    )


def part_dot(a, b):
    return lax.dot_general(a, b, NN, preferred_element_type=jnp.float32)


def split(x):
    high = x.astype(jnp.bfloat16)
    rest = x - high.astype(jnp.float32)
    mid = rest.astype(jnp.bfloat16)
    low = (rest - mid.astype(jnp.float32)).astype(jnp.bfloat16)
    return high, mid, low


def block_of(ref, index):
    return ref[index * B:(index + 1) * B, :]


def gram_kernel(half_ref, a_ref, *refs):
    before, out_ref = refs if len(refs) == 2 else (None, refs[0])
    left_lanes = lax.broadcasted_iota(jnp.int32, (H, B), 1) < H

    def put(index, value):
        if before is not None:
            value = value + block_of(before, index)
        out_ref[index * B:(index + 1) * B, :] = value

    def fill(half):
        order = []
        for tile in TILES[half]:
            order += [(tile, tile)] + [(other, tile) for other in range(tile)]
        ready, diagonal = {}, {}

        def take(tile):
            if tile not in ready:
                value = a_ref[:, T * tile:T * (tile + 1)]
                ready[tile] = split(value.T), split(value)
            return ready[tile]

        for row, column in order:
            right, left = take(column)[1], take(row)[0]
            gram = part_dot(left[2], right[0]) + part_dot(left[1], right[1])
            gram = gram + part_dot(left[0], right[2])
            gram = gram + (part_dot(left[1], right[0]) + part_dot(left[0], right[1]))
            gram = gram + part_dot(left[0], right[0])
            for r in range(2):
                for c in range(2):
                    pair = (2 * row + r, 2 * column + c)
                    block = gram[r * B:(r + 1) * B, c * B:(c + 1) * B]
                    if pair in DIAGONAL[half]:
                        diagonal[pair] = block
                    elif pair in ABOVE[half]:
                        put(ABOVE[half].index(pair), block)
        *hosts, last = [diagonal[pair] for pair in DIAGONAL[half]]
        guests = (last[:H], pltpu.roll(last[:H], H, 1), pltpu.roll(last[H:], H, 1))
        for index, (block, guest) in enumerate(zip(hosts, guests)):
            lower = jnp.where(left_lanes, guest, block[H:])
            put(len(ABOVE[half]) + index, jnp.concatenate([block[:H], lower], axis=0))

    for half in range(2):
        pl.when(half_ref[0] == half)(functools.partial(fill, half))


def gram_half(half, a, *before):
    vmem = pl.BlockSpec(memory_space=pltpu.VMEM)
    return pl.pallas_call(
        gram_kernel,
        out_shape=jax.ShapeDtypeStruct((PACKED * B, B), jnp.float32),
        in_specs=[pl.BlockSpec(memory_space=pltpu.SMEM), vmem] + [vmem] * len(before),
        out_specs=vmem,
        compiler_params=pltpu.CompilerParams(vmem_limit_bytes=24 * 1024 * 1024),
        cost_estimate=pl.CostEstimate(
            flops=6 * 2 * 256 * 1280 * 256, bytes_accessed=2300000, transcendentals=0
        ),
        name="gram_half",
    )(half, a, *before)


def unpack(half, blocks):
    count = len(ABOVE[half])
    low_rows = lax.broadcasted_iota(jnp.int32, (B, B), 0) >= H
    left = lax.broadcasted_iota(jnp.int32, (B, B), 1) < H
    guests = [block[H:] for block in blocks[count:]]
    upper = jnp.where(left[:H], guests[0], pltpu.roll(guests[1], H, 1))
    last = jnp.concatenate([upper, pltpu.roll(guests[2], H, 1)], axis=0)
    for pair, block in zip(ABOVE[half], blocks):
        yield pair, block
    for pair, block in zip(DIAGONAL[half], list(blocks[count:]) + [last]):
        yield pair, jnp.where(low_rows & left, block.T, block)


def inverse_factor(gram, width=4):
    k = gram.shape[0]
    rows = k // 8
    wide = jnp.concatenate([gram, jnp.zeros((k, B - k), jnp.float32)], axis=1)
    tiles = [wide[8 * t:8 * t + 8, :] for t in range(rows)]
    lane = lax.broadcasted_iota(jnp.int32, (8, B), 1)
    sub = lax.broadcasted_iota(jnp.int32, (8, B), 0)

    def row_of(tile, s):
        return jnp.broadcast_to(tile[s:s + 1, :], (8, B))

    def columns(start, first):
        return [
            {u: jnp.broadcast_to(tiles[u][:, c:c + 1], (8, B)) for u in range(first, rows)}
            for c in range(start, min(start + width, k))
        ]

    scale = [None] * rows
    now = columns(0, 0)
    for start in range(0, k, width):
        t, top = divmod(start, 8)
        ahead = columns(start + width, t)
        inside = (lane >= start) & (lane < start + width)
        unit = jnp.where(lane == sub + 8 * t, 1.0, 0.0)
        tiles[t] = jnp.where(inside & (sub >= top), unit, tiles[t])
        n = len(now)
        own = {(a, b): row_of(now[b][t], top + a) for a in range(n) for b in range(a + 1)}
        inverse, lower = [], {}
        for c in range(n):
            inverse.append(1.0 / own[c, c])
            root = lax.rsqrt(own[c, c])
            scale[t] = root if top + c == 0 else jnp.where(sub == top + c, root, scale[t])
            for a in range(c + 1, n):
                lower[a, c] = own[a, c] * inverse[c]
                for b in range(c + 1, a + 1):
                    own[a, b] = own[a, b] - lower[a, c] * own[b, c]
        ratios, lines = [], []
        for c in range(n):
            for o in range(c + 1, n):
                now[o][t] = now[o][t] - now[c][t] * lower[o, c]
            ratios.append([row_of(other[t], top + c) * inverse[c] for other in ahead])
            lines.append(row_of(tiles[t], top + c) * inverse[c])
            for other, ratio in zip(ahead, ratios[c]):
                other[t] = other[t] - now[c][t] * ratio
            tiles[t] = tiles[t] - jnp.where(sub > top + c, now[c][t], 0.0) * lines[c]
        for u in range(t + 1, rows):
            tiles[u] = jnp.where(inside, 0.0, tiles[u])
            for c in range(n):
                for o in range(c + 1, n):
                    now[o][u] = now[o][u] - now[c][u] * lower[o, c]
                for other, ratio in zip(ahead, ratios[c]):
                    other[u] = other[u] - now[c][u] * ratio
                tiles[u] = tiles[u] - now[c][u] * lines[c]
        now = ahead
    out = [jnp.where(lane <= sub + 8 * t, tiles[t], 0.0) * scale[t] for t in range(rows)]
    return jnp.concatenate(out, axis=0)[:, :k]


def times_gram(xt, parts):
    k, d = xt.shape
    p = -(-k // 16) * 16
    padded = jnp.concatenate([xt, jnp.zeros((p - k, d), jnp.float32)], axis=0)
    stack = jnp.concatenate(split(padded), axis=0)
    high = part_dot(stack, parts[0][...])
    mid = part_dot(stack[:2 * p], parts[1][...])
    low = part_dot(stack[:p], parts[2][...])
    out = (low + mid[p:] + high[2 * p:]) + (mid[:p] + high[p:2 * p]) + high[:p]
    return out[:k]


def fill_parts(half, packed, parts):
    blocks = [block_of(packed, index) for index in range(PACKED)]
    for (i, j), block in unpack(half, blocks):
        for part, value in zip(parts, split(block)):
            part[i * B:(i + 1) * B, j * B:(j + 1) * B] = value
        if i < j:
            for part, value in zip(parts, split(block.T)):
                part[j * B:(j + 1) * B, i * B:(i + 1) * B] = value


def iterate_kernel(total, core_ref, own_ref, other_ref, xt_ref, a_ref, rowt_ref, proj_ref, *parts):
    first = core_ref[0] == 0
    fill_parts(0, jnp.where(first, own_ref[...], other_ref[...]), parts)
    fill_parts(1, jnp.where(first, other_ref[...], own_ref[...]), parts)
    root = math.sqrt(total)
    xt = xt_ref[...]
    for step in range(ITERS + 1):
        zt = times_gram(xt, parts)
        gram = dot(xt, zt, NT)
        if step == ITERS:
            yt = dot(xt, a_ref[...], NT)
        inv = inverse_factor(gram)
        crosst = dot(inv, zt)
        if step < ITERS:
            xt = dot(inverse_factor(dot(crosst, crosst, NT)), crosst)
    proj_ref[...] = crosst / root
    rowt_ref[...] = dot(inv, yt) * root


def iterate(total, core, own, other, xt, a):
    k, d = xt.shape
    vmem = pl.BlockSpec(memory_space=pltpu.VMEM)
    return pl.pallas_call(
        functools.partial(iterate_kernel, total),
        out_shape=(
            jax.ShapeDtypeStruct((k, a.shape[0]), jnp.float32),
            jax.ShapeDtypeStruct((k, d), jnp.float32),
        ),
        in_specs=[pl.BlockSpec(memory_space=pltpu.SMEM)] + [vmem] * 4,
        out_specs=(vmem, vmem),
        scratch_shapes=[pltpu.VMEM((d, d), jnp.bfloat16)] * 3,
        compiler_params=pltpu.CompilerParams(vmem_limit_bytes=32 * 1024 * 1024),
        name="iterate",
    )(core, own, other, xt, a)


def exchange(v, groups):
    return lax.all_to_all(v, "device", 0, 0, axis_index_groups=groups, tiled=True)


def scatter_sum(v, groups):
    return jnp.sum(exchange(v.reshape(len(groups[0]), -1, B), groups), axis=0)


def collect(v, groups):
    copies = jnp.broadcast_to(v[None], (len(groups[0]),) + v.shape)
    return exchange(copies, groups)


def all_sum(v):
    v = scatter_sum(v, NEAR)
    for groups in FAR:
        v = jnp.sum(collect(v, groups), axis=0)
    return collect(v, NEAR).reshape(-1, B)


def swap(v):
    return lax.ppermute(v, "device", SWAP)


def local(total, slab, test_matrix):
    core = (lax.axis_index("device") // X % 2).astype(jnp.int32)[None]
    there = swap(slab)
    own = all_sum(gram_half(core, there, gram_half(core, slab)))
    rowt, projected = iterate(total, core, own, swap(own), test_matrix.T, slab)
    return rowt.T, projected


def solution(mesh):
    flat = Mesh(mesh.devices.reshape(-1), ("device",))
    rows = P("device", None)

    def run(slab, test_matrix):
        return jax.shard_map(
            functools.partial(local, slab.shape[0]),
            mesh=flat,
            in_specs=(rows, P()),
            out_specs=(rows, P()),
            check_vma=False,
        )(slab, test_matrix)

    return run
```

```python
import functools
import math

import jax
import jax.numpy as jnp
from jax import lax
from jax.experimental import pallas as pl
from jax.experimental.pallas import tpu as pltpu
from jax.sharding import Mesh, PartitionSpec as P

ITERS = 2
B = 128
T = 256
AXES = ("y", "y_pair", "z", "z_pair", "core", "x")
NEAR = ("y_pair", "z_pair", "x")
FAR = ("z",), ("y",)

NT = (((1,), (1,)), ((), ()))
NN = (((1,), (0,)), ((), ()))

TILES = ((0, 3), (1, 2))
PAIRS = tuple(
    tuple((i, j) for tile in tiles for j in (2 * tile, 2 * tile + 1) for i in range(j + 1))
    for tiles in TILES
)
ABOVE = tuple(tuple(pair for pair in pairs if pair[0] < pair[1]) for pairs in PAIRS)
DIAGONAL = tuple(tuple(pair for pair in pairs if pair[0] == pair[1]) for pairs in PAIRS)
PACKED = len(ABOVE[0]) + len(DIAGONAL[0]) - 1
H = B // 2


def dot(a, b, dims=NN):
    return lax.dot_general(
        a, b, dims, precision=lax.Precision.HIGHEST, preferred_element_type=jnp.float32
    )


def part_dot(a, b):
    return lax.dot_general(a, b, NN, preferred_element_type=jnp.float32)


def split(x):
    high = x.astype(jnp.bfloat16)
    rest = x - high.astype(jnp.float32)
    mid = rest.astype(jnp.bfloat16)
    low = (rest - mid.astype(jnp.float32)).astype(jnp.bfloat16)
    return high, mid, low


def block_of(ref, index):
    return ref[index * B:(index + 1) * B, :]


def gram_kernel(half_ref, a_ref, *refs):
    before, out_ref = refs if len(refs) == 2 else (None, refs[0])
    left_lanes = lax.broadcasted_iota(jnp.int32, (H, B), 1) < H

    def put(index, value):
        if before is not None:
            value = value + block_of(before, index)
        out_ref[index * B:(index + 1) * B, :] = value

    def fill(half):
        order = []
        for tile in TILES[half]:
            order += [(tile, tile)] + [(other, tile) for other in range(tile)]
        ready, diagonal = {}, {}

        def take(tile):
            if tile not in ready:
                value = a_ref[:, T * tile:T * (tile + 1)]
                ready[tile] = split(value.T), split(value)
            return ready[tile]

        for row, column in order:
            right, left = take(column)[1], take(row)[0]
            gram = part_dot(left[2], right[0]) + part_dot(left[1], right[1])
            gram = gram + part_dot(left[0], right[2])
            gram = gram + (part_dot(left[1], right[0]) + part_dot(left[0], right[1]))
            gram = gram + part_dot(left[0], right[0])
            for r in range(2):
                for c in range(2):
                    pair = (2 * row + r, 2 * column + c)
                    block = gram[r * B:(r + 1) * B, c * B:(c + 1) * B]
                    if pair in DIAGONAL[half]:
                        diagonal[pair] = block
                    elif pair in ABOVE[half]:
                        put(ABOVE[half].index(pair), block)
        *hosts, last = [diagonal[pair] for pair in DIAGONAL[half]]
        guests = (last[:H], pltpu.roll(last[:H], H, 1), pltpu.roll(last[H:], H, 1))
        for index, (block, guest) in enumerate(zip(hosts, guests)):
            lower = jnp.where(left_lanes, guest, block[H:])
            put(len(ABOVE[half]) + index, jnp.concatenate([block[:H], lower], axis=0))

    for half in range(2):
        pl.when(half_ref[0] == half)(functools.partial(fill, half))


def gram_half(half, a, *before):
    vmem = pl.BlockSpec(memory_space=pltpu.VMEM)
    return pl.pallas_call(
        gram_kernel,
        out_shape=jax.ShapeDtypeStruct((PACKED * B, B), jnp.float32),
        in_specs=[pl.BlockSpec(memory_space=pltpu.SMEM), vmem] + [vmem] * len(before),
        out_specs=vmem,
        compiler_params=pltpu.CompilerParams(vmem_limit_bytes=24 * 1024 * 1024),
        cost_estimate=pl.CostEstimate(
            flops=6 * 2 * 256 * 1280 * 256, bytes_accessed=2300000, transcendentals=0
        ),
        name="gram_half",
    )(half, a, *before)


def unpack(half, blocks):
    count = len(ABOVE[half])
    low_rows = lax.broadcasted_iota(jnp.int32, (B, B), 0) >= H
    left = lax.broadcasted_iota(jnp.int32, (B, B), 1) < H
    guests = [block[H:] for block in blocks[count:]]
    upper = jnp.where(left[:H], guests[0], pltpu.roll(guests[1], H, 1))
    last = jnp.concatenate([upper, pltpu.roll(guests[2], H, 1)], axis=0)
    for pair, block in zip(ABOVE[half], blocks):
        yield pair, block
    for pair, block in zip(DIAGONAL[half], list(blocks[count:]) + [last]):
        yield pair, jnp.where(low_rows & left, block.T, block)


def inverse_factor(gram, width=4):
    k = gram.shape[0]
    rows = k // 8
    wide = jnp.concatenate([gram, jnp.zeros((k, B - k), jnp.float32)], axis=1)
    tiles = [wide[8 * t:8 * t + 8, :] for t in range(rows)]
    lane = lax.broadcasted_iota(jnp.int32, (8, B), 1)
    sub = lax.broadcasted_iota(jnp.int32, (8, B), 0)

    def row_of(tile, s):
        return jnp.broadcast_to(tile[s:s + 1, :], (8, B))

    def columns(start, first):
        return [
            {u: jnp.broadcast_to(tiles[u][:, c:c + 1], (8, B)) for u in range(first, rows)}
            for c in range(start, min(start + width, k))
        ]

    scale = [None] * rows
    now = columns(0, 0)
    for start in range(0, k, width):
        t, top = divmod(start, 8)
        ahead = columns(start + width, t)
        inside = (lane >= start) & (lane < start + width)
        unit = jnp.where(lane == sub + 8 * t, 1.0, 0.0)
        tiles[t] = jnp.where(inside & (sub >= top), unit, tiles[t])
        n = len(now)
        own = {(a, b): row_of(now[b][t], top + a) for a in range(n) for b in range(a + 1)}
        inverse, lower = [], {}
        for c in range(n):
            inverse.append(1.0 / own[c, c])
            root = lax.rsqrt(own[c, c])
            scale[t] = root if top + c == 0 else jnp.where(sub == top + c, root, scale[t])
            for a in range(c + 1, n):
                lower[a, c] = own[a, c] * inverse[c]
                for b in range(c + 1, a + 1):
                    own[a, b] = own[a, b] - lower[a, c] * own[b, c]
        ratios, lines = [], []
        for c in range(n):
            for o in range(c + 1, n):
                now[o][t] = now[o][t] - now[c][t] * lower[o, c]
            ratios.append([row_of(other[t], top + c) * inverse[c] for other in ahead])
            lines.append(row_of(tiles[t], top + c) * inverse[c])
            for other, ratio in zip(ahead, ratios[c]):
                other[t] = other[t] - now[c][t] * ratio
            tiles[t] = tiles[t] - jnp.where(sub > top + c, now[c][t], 0.0) * lines[c]
        for u in range(t + 1, rows):
            tiles[u] = jnp.where(inside, 0.0, tiles[u])
            for c in range(n):
                for o in range(c + 1, n):
                    now[o][u] = now[o][u] - now[c][u] * lower[o, c]
                for other, ratio in zip(ahead, ratios[c]):
                    other[u] = other[u] - now[c][u] * ratio
                tiles[u] = tiles[u] - now[c][u] * lines[c]
        now = ahead
    out = [jnp.where(lane <= sub + 8 * t, tiles[t], 0.0) * scale[t] for t in range(rows)]
    return jnp.concatenate(out, axis=0)[:, :k]


def times_gram(xt, parts):
    k, d = xt.shape
    p = -(-k // 16) * 16
    padded = jnp.concatenate([xt, jnp.zeros((p - k, d), jnp.float32)], axis=0)
    stack = jnp.concatenate(split(padded), axis=0)
    high = part_dot(stack, parts[0][...])
    mid = part_dot(stack[:2 * p], parts[1][...])
    low = part_dot(stack[:p], parts[2][...])
    out = (low + mid[p:] + high[2 * p:]) + (mid[:p] + high[p:2 * p]) + high[:p]
    return out[:k]


def fill_parts(half, packed, parts):
    blocks = [block_of(packed, index) for index in range(PACKED)]
    for (i, j), block in unpack(half, blocks):
        for part, value in zip(parts, split(block)):
            part[i * B:(i + 1) * B, j * B:(j + 1) * B] = value
        if i < j:
            for part, value in zip(parts, split(block.T)):
                part[j * B:(j + 1) * B, i * B:(i + 1) * B] = value


def iterate_kernel(total, core_ref, own_ref, other_ref, xt_ref, a_ref, rowt_ref, proj_ref, *parts):
    first = core_ref[0] == 0
    fill_parts(0, jnp.where(first, own_ref[...], other_ref[...]), parts)
    fill_parts(1, jnp.where(first, other_ref[...], own_ref[...]), parts)
    root = math.sqrt(total)
    xt = xt_ref[...]
    zt = times_gram(xt, parts)
    for step in range(ITERS + 1):
        gram = dot(xt, zt, NT)
        if step == ITERS:
            yt = dot(xt, a_ref[...], NT)
        inv = inverse_factor(gram)
        crosst = dot(inv, zt)
        if step == ITERS:
            break
        square = dot(crosst, crosst, NT)
        if step == 0:
            ahead = times_gram(crosst, parts)
        inv = inverse_factor(square)
        xt = dot(inv, crosst)
        zt = dot(inv, ahead) if step == 0 else times_gram(xt, parts)
    proj_ref[...] = crosst / root
    rowt_ref[...] = dot(inv, yt) * root


def iterate(total, core, own, other, xt, a):
    k, d = xt.shape
    vmem = pl.BlockSpec(memory_space=pltpu.VMEM)
    return pl.pallas_call(
        functools.partial(iterate_kernel, total),
        out_shape=(
            jax.ShapeDtypeStruct((k, a.shape[0]), jnp.float32),
            jax.ShapeDtypeStruct((k, d), jnp.float32),
        ),
        in_specs=[pl.BlockSpec(memory_space=pltpu.SMEM)] + [vmem] * 4,
        out_specs=(vmem, vmem),
        scratch_shapes=[pltpu.VMEM((d, d), jnp.bfloat16)] * 3,
        compiler_params=pltpu.CompilerParams(vmem_limit_bytes=32 * 1024 * 1024),
        name="iterate",
    )(core, own, other, xt, a)


def scatter_sum(v, axes):
    v = v.reshape(lax.axis_size(axes), -1, B)
    return jnp.sum(lax.all_to_all(v, axes, 0, 0, tiled=True), axis=0)


def collect(v, axes):
    copies = jnp.broadcast_to(v[None], (lax.axis_size(axes),) + v.shape)
    return lax.all_to_all(copies, axes, 0, 0, tiled=True)


def all_sum(v):
    v = scatter_sum(v, NEAR)
    for axes in FAR:
        v = jnp.sum(collect(v, axes), axis=0)
    return collect(v, NEAR).reshape(-1, B)


def swap(v):
    return lax.ppermute(v, "core", [(0, 1), (1, 0)])


def local(total, slab, test_matrix):
    core = lax.axis_index("core").astype(jnp.int32)[None]
    there = swap(slab)
    own = all_sum(gram_half(core, there, gram_half(core, slab)))
    rowt, projected = iterate(total, core, own, swap(own), test_matrix.T, slab)
    return rowt.T, projected


def solution(mesh):
    fine = Mesh(mesh.devices.reshape(4, 2, 4, 2, 2, 4), AXES)
    rows = P(AXES, None)

    def run(slab, test_matrix):
        return jax.shard_map(
            functools.partial(local, slab.shape[0]),
            mesh=fine,
            in_specs=(rows, P()),
            out_specs=(rows, P()),
            check_vma=False,
        )(slab, test_matrix)

    return run
```

```python
import functools
import math

import jax
import jax.numpy as jnp
from jax import lax
from jax.experimental import pallas as pl
from jax.experimental.pallas import tpu as pltpu
from jax.sharding import Mesh, PartitionSpec as P

ITERS = 2
B = 128
T = 256
X, Y, Z = 4, 8, 8


def device(y, z, core, x):
    return ((y % Y * Z + z % Z) * 2 + core) * X + x % X


NEAR = [
    [device(y + a, z + b, core, x) for a in range(2) for b in range(2) for x in range(X)]
    for core in range(2) for y in range(0, Y, 2) for z in range(0, Z, 2)
]


def along_z(core):
    return [
        [device(y, z + a, core, x) for z in range(0, Z, 2)]
        for y in range(Y) for x in range(X) for a in range(2)
    ]


def along_y(core):
    return [
        [device(y + a, z, core, x) for y in range(0, Y, 2)]
        for z in range(Z) for x in range(X) for a in range(2)
    ]


FAR = along_z(0) + along_y(1), along_y(0) + along_z(1)
SWAP = [
    (device(y, z, core, x), device(y, z, 1 - core, x))
    for y in range(Y) for z in range(Z) for core in range(2) for x in range(X)
]

NT = (((1,), (1,)), ((), ()))
NN = (((1,), (0,)), ((), ()))

TILES = ((0, 3), (1, 2))
PAIRS = tuple(
    tuple((i, j) for tile in tiles for j in (2 * tile, 2 * tile + 1) for i in range(j + 1))
    for tiles in TILES
)
ABOVE = tuple(tuple(pair for pair in pairs if pair[0] < pair[1]) for pairs in PAIRS)
DIAGONAL = tuple(tuple(pair for pair in pairs if pair[0] == pair[1]) for pairs in PAIRS)
PACKED = len(ABOVE[0]) + len(DIAGONAL[0]) - 1
H = B // 2


def dot(a, b, dims=NN):
    return lax.dot_general(
        a, b, dims, precision=lax.Precision.HIGHEST, preferred_element_type=jnp.float32
    )


def part_dot(a, b):
    return lax.dot_general(a, b, NN, preferred_element_type=jnp.float32)


def split(x):
    high = x.astype(jnp.bfloat16)
    rest = x - high.astype(jnp.float32)
    mid = rest.astype(jnp.bfloat16)
    low = (rest - mid.astype(jnp.float32)).astype(jnp.bfloat16)
    return high, mid, low


def block_of(ref, index):
    return ref[index * B:(index + 1) * B, :]


def gram_kernel(half_ref, a_ref, *refs):
    before, out_ref = refs if len(refs) == 2 else (None, refs[0])
    left_lanes = lax.broadcasted_iota(jnp.int32, (H, B), 1) < H

    def put(index, value):
        if before is not None:
            value = value + block_of(before, index)
        out_ref[index * B:(index + 1) * B, :] = value

    def fill(half):
        order = []
        for tile in TILES[half]:
            order += [(tile, tile)] + [(other, tile) for other in range(tile)]
        ready, diagonal = {}, {}

        def take(tile):
            if tile not in ready:
                value = a_ref[:, T * tile:T * (tile + 1)]
                ready[tile] = split(value.T), split(value)
            return ready[tile]

        for row, column in order:
            right, left = take(column)[1], take(row)[0]
            gram = part_dot(left[2], right[0]) + part_dot(left[1], right[1])
            gram = gram + part_dot(left[0], right[2])
            gram = gram + (part_dot(left[1], right[0]) + part_dot(left[0], right[1]))
            gram = gram + part_dot(left[0], right[0])
            for r in range(2):
                for c in range(2):
                    pair = (2 * row + r, 2 * column + c)
                    block = gram[r * B:(r + 1) * B, c * B:(c + 1) * B]
                    if pair in DIAGONAL[half]:
                        diagonal[pair] = block
                    elif pair in ABOVE[half]:
                        put(ABOVE[half].index(pair), block)
        *hosts, last = [diagonal[pair] for pair in DIAGONAL[half]]
        guests = (last[:H], pltpu.roll(last[:H], H, 1), pltpu.roll(last[H:], H, 1))
        for index, (block, guest) in enumerate(zip(hosts, guests)):
            lower = jnp.where(left_lanes, guest, block[H:])
            put(len(ABOVE[half]) + index, jnp.concatenate([block[:H], lower], axis=0))

    for half in range(2):
        pl.when(half_ref[0] == half)(functools.partial(fill, half))


def gram_half(half, a, *before):
    vmem = pl.BlockSpec(memory_space=pltpu.VMEM)
    return pl.pallas_call(
        gram_kernel,
        out_shape=jax.ShapeDtypeStruct((PACKED * B, B), jnp.float32),
        in_specs=[pl.BlockSpec(memory_space=pltpu.SMEM), vmem] + [vmem] * len(before),
        out_specs=vmem,
        compiler_params=pltpu.CompilerParams(vmem_limit_bytes=24 * 1024 * 1024),
        cost_estimate=pl.CostEstimate(
            flops=6 * 2 * 256 * 1280 * 256, bytes_accessed=2300000, transcendentals=0
        ),
        name="gram_half",
    )(half, a, *before)


def unpack(half, blocks):
    count = len(ABOVE[half])
    low_rows = lax.broadcasted_iota(jnp.int32, (B, B), 0) >= H
    left = lax.broadcasted_iota(jnp.int32, (B, B), 1) < H
    guests = [block[H:] for block in blocks[count:]]
    upper = jnp.where(left[:H], guests[0], pltpu.roll(guests[1], H, 1))
    last = jnp.concatenate([upper, pltpu.roll(guests[2], H, 1)], axis=0)
    for pair, block in zip(ABOVE[half], blocks):
        yield pair, block
    for pair, block in zip(DIAGONAL[half], list(blocks[count:]) + [last]):
        yield pair, jnp.where(low_rows & left, block.T, block)


def inverse_factor(gram, width=4):
    k = gram.shape[0]
    rows = k // 8
    wide = jnp.concatenate([gram, jnp.zeros((k, B - k), jnp.float32)], axis=1)
    tiles = [wide[8 * t:8 * t + 8, :] for t in range(rows)]
    lane = lax.broadcasted_iota(jnp.int32, (8, B), 1)
    sub = lax.broadcasted_iota(jnp.int32, (8, B), 0)

    def row_of(tile, s):
        return jnp.broadcast_to(tile[s:s + 1, :], (8, B))

    def columns(start, first):
        return [
            {u: jnp.broadcast_to(tiles[u][:, c:c + 1], (8, B)) for u in range(first, rows)}
            for c in range(start, min(start + width, k))
        ]

    scale = [None] * rows
    now = columns(0, 0)
    for start in range(0, k, width):
        t, top = divmod(start, 8)
        ahead = columns(start + width, t)
        inside = (lane >= start) & (lane < start + width)
        unit = jnp.where(lane == sub + 8 * t, 1.0, 0.0)
        tiles[t] = jnp.where(inside & (sub >= top), unit, tiles[t])
        n = len(now)
        own = {(a, b): row_of(now[b][t], top + a) for a in range(n) for b in range(a + 1)}
        inverse, lower = [], {}
        for c in range(n):
            inverse.append(1.0 / own[c, c])
            root = lax.rsqrt(own[c, c])
            scale[t] = root if top + c == 0 else jnp.where(sub == top + c, root, scale[t])
            for a in range(c + 1, n):
                lower[a, c] = own[a, c] * inverse[c]
                for b in range(c + 1, a + 1):
                    own[a, b] = own[a, b] - lower[a, c] * own[b, c]
        ratios, lines = [], []
        for c in range(n):
            for o in range(c + 1, n):
                now[o][t] = now[o][t] - now[c][t] * lower[o, c]
            ratios.append([row_of(other[t], top + c) * inverse[c] for other in ahead])
            lines.append(row_of(tiles[t], top + c) * inverse[c])
            for other, ratio in zip(ahead, ratios[c]):
                other[t] = other[t] - now[c][t] * ratio
            tiles[t] = tiles[t] - jnp.where(sub > top + c, now[c][t], 0.0) * lines[c]
        for u in range(t + 1, rows):
            tiles[u] = jnp.where(inside, 0.0, tiles[u])
            for c in range(n):
                for o in range(c + 1, n):
                    now[o][u] = now[o][u] - now[c][u] * lower[o, c]
                for other, ratio in zip(ahead, ratios[c]):
                    other[u] = other[u] - now[c][u] * ratio
                tiles[u] = tiles[u] - now[c][u] * lines[c]
        now = ahead
    out = [jnp.where(lane <= sub + 8 * t, tiles[t], 0.0) * scale[t] for t in range(rows)]
    return jnp.concatenate(out, axis=0)[:, :k]


def times_gram(xt, parts):
    k, d = xt.shape
    p = -(-k // 16) * 16
    padded = jnp.concatenate([xt, jnp.zeros((p - k, d), jnp.float32)], axis=0)
    stack = jnp.concatenate(split(padded), axis=0)
    high = part_dot(stack, parts[0][...])
    mid = part_dot(stack[:2 * p], parts[1][...])
    low = part_dot(stack[:p], parts[2][...])
    out = (low + mid[p:] + high[2 * p:]) + (mid[:p] + high[p:2 * p]) + high[:p]
    return out[:k]


def fill_parts(half, packed, parts):
    blocks = [block_of(packed, index) for index in range(PACKED)]
    for (i, j), block in unpack(half, blocks):
        for part, value in zip(parts, split(block)):
            part[i * B:(i + 1) * B, j * B:(j + 1) * B] = value
        if i < j:
            for part, value in zip(parts, split(block.T)):
                part[j * B:(j + 1) * B, i * B:(i + 1) * B] = value


def iterate_kernel(total, core_ref, own_ref, other_ref, xt_ref, a_ref, rowt_ref, proj_ref, *parts):
    first = core_ref[0] == 0
    fill_parts(0, jnp.where(first, own_ref[...], other_ref[...]), parts)
    fill_parts(1, jnp.where(first, other_ref[...], own_ref[...]), parts)
    root = math.sqrt(total)
    xt = xt_ref[...]
    zt = times_gram(xt, parts)
    for step in range(ITERS + 1):
        gram = dot(xt, zt, NT)
        if step == ITERS:
            yt = dot(xt, a_ref[...], NT)
        inv = inverse_factor(gram)
        crosst = dot(inv, zt)
        if step == ITERS:
            break
        square = dot(crosst, crosst, NT)
        if step == 0:
            ahead = times_gram(crosst, parts)
        inv = inverse_factor(square)
        xt = dot(inv, crosst)
        zt = dot(inv, ahead) if step == 0 else times_gram(xt, parts)
    proj_ref[...] = crosst / root
    rowt_ref[...] = dot(inv, yt) * root


def iterate(total, core, own, other, xt, a):
    k, d = xt.shape
    vmem = pl.BlockSpec(memory_space=pltpu.VMEM)
    return pl.pallas_call(
        functools.partial(iterate_kernel, total),
        out_shape=(
            jax.ShapeDtypeStruct((k, a.shape[0]), jnp.float32),
            jax.ShapeDtypeStruct((k, d), jnp.float32),
        ),
        in_specs=[pl.BlockSpec(memory_space=pltpu.SMEM)] + [vmem] * 4,
        out_specs=(vmem, vmem),
        scratch_shapes=[pltpu.VMEM((d, d), jnp.bfloat16)] * 3,
        compiler_params=pltpu.CompilerParams(vmem_limit_bytes=32 * 1024 * 1024),
        name="iterate",
    )(core, own, other, xt, a)


def exchange(v, groups):
    return lax.all_to_all(v, "device", 0, 0, axis_index_groups=groups, tiled=True)


def scatter_sum(v, groups):
    return jnp.sum(exchange(v.reshape(len(groups[0]), -1, B), groups), axis=0)


def collect(v, groups):
    copies = jnp.broadcast_to(v[None], (len(groups[0]),) + v.shape)
    return exchange(copies, groups)


def all_sum(v):
    v = scatter_sum(v, NEAR)
    for groups in FAR:
        v = jnp.sum(collect(v, groups), axis=0)
    return collect(v, NEAR).reshape(-1, B)


def swap(v):
    return lax.ppermute(v, "device", SWAP)


def local(total, slab, test_matrix):
    core = (lax.axis_index("device") // X % 2).astype(jnp.int32)[None]
    there = swap(slab)
    own = all_sum(gram_half(core, there, gram_half(core, slab)))
    rowt, projected = iterate(total, core, own, swap(own), test_matrix.T, slab)
    return rowt.T, projected


def solution(mesh):
    flat = Mesh(mesh.devices.reshape(-1), ("device",))
    rows = P("device", None)

    def run(slab, test_matrix):
        return jax.shard_map(
            functools.partial(local, slab.shape[0]),
            mesh=flat,
            in_specs=(rows, P()),
            out_specs=(rows, P()),
            check_vma=False,
        )(slab, test_matrix)

    return run
```

```python
import functools
import math

import jax
import jax.numpy as jnp
from jax import lax
from jax.experimental import pallas as pl
from jax.experimental.pallas import tpu as pltpu
from jax.sharding import Mesh, PartitionSpec as P

ITERS = 2
B = 128
T = 256
AXES = ("y", "y_pair", "z", "z_pair", "core", "x")
NEAR = ("x", "y_pair", "z_pair")
FAR = ("z",), ("y",)

NT = (((1,), (1,)), ((), ()))
NN = (((1,), (0,)), ((), ()))

TILES = ((0, 3), (1, 2))
PAIRS = tuple(
    tuple((i, j) for tile in tiles for j in (2 * tile, 2 * tile + 1) for i in range(j + 1))
    for tiles in TILES
)
ABOVE = tuple(tuple(pair for pair in pairs if pair[0] < pair[1]) for pairs in PAIRS)
DIAGONAL = tuple(tuple(pair for pair in pairs if pair[0] == pair[1]) for pairs in PAIRS)
PACKED = len(ABOVE[0]) + len(DIAGONAL[0]) - 1
H = B // 2


def dot(a, b, dims=NN):
    return lax.dot_general(
        a, b, dims, precision=lax.Precision.HIGHEST, preferred_element_type=jnp.float32
    )


def part_dot(a, b):
    return lax.dot_general(a, b, NN, preferred_element_type=jnp.float32)


def split(x):
    high = x.astype(jnp.bfloat16)
    rest = x - high.astype(jnp.float32)
    mid = rest.astype(jnp.bfloat16)
    low = (rest - mid.astype(jnp.float32)).astype(jnp.bfloat16)
    return high, mid, low


def block_of(ref, index):
    return ref[index * B:(index + 1) * B, :]


def gram_kernel(half_ref, a_ref, *refs):
    before, out_ref = refs if len(refs) == 2 else (None, refs[0])
    left_lanes = lax.broadcasted_iota(jnp.int32, (H, B), 1) < H

    def put(index, value):
        if before is not None:
            value = value + block_of(before, index)
        out_ref[index * B:(index + 1) * B, :] = value

    def fill(half):
        order = []
        for tile in TILES[half]:
            order += [(tile, tile)] + [(other, tile) for other in range(tile)]
        ready, diagonal = {}, {}

        def take(tile):
            if tile not in ready:
                value = a_ref[:, T * tile:T * (tile + 1)]
                ready[tile] = split(value.T), split(value)
            return ready[tile]

        for row, column in order:
            right, left = take(column)[1], take(row)[0]
            gram = part_dot(left[2], right[0]) + part_dot(left[1], right[1])
            gram = gram + part_dot(left[0], right[2])
            gram = gram + (part_dot(left[1], right[0]) + part_dot(left[0], right[1]))
            gram = gram + part_dot(left[0], right[0])
            for r in range(2):
                for c in range(2):
                    pair = (2 * row + r, 2 * column + c)
                    block = gram[r * B:(r + 1) * B, c * B:(c + 1) * B]
                    if pair in DIAGONAL[half]:
                        diagonal[pair] = block
                    elif pair in ABOVE[half]:
                        put(ABOVE[half].index(pair), block)
        *hosts, last = [diagonal[pair] for pair in DIAGONAL[half]]
        guests = (last[:H], pltpu.roll(last[:H], H, 1), pltpu.roll(last[H:], H, 1))
        for index, (block, guest) in enumerate(zip(hosts, guests)):
            lower = jnp.where(left_lanes, guest, block[H:])
            put(len(ABOVE[half]) + index, jnp.concatenate([block[:H], lower], axis=0))

    for half in range(2):
        pl.when(half_ref[0] == half)(functools.partial(fill, half))


def gram_half(half, a, *before):
    vmem = pl.BlockSpec(memory_space=pltpu.VMEM)
    return pl.pallas_call(
        gram_kernel,
        out_shape=jax.ShapeDtypeStruct((PACKED * B, B), jnp.float32),
        in_specs=[pl.BlockSpec(memory_space=pltpu.SMEM), vmem] + [vmem] * len(before),
        out_specs=vmem,
        compiler_params=pltpu.CompilerParams(vmem_limit_bytes=24 * 1024 * 1024),
        cost_estimate=pl.CostEstimate(
            flops=6 * 2 * 256 * 1280 * 256, bytes_accessed=2300000, transcendentals=0
        ),
        name="gram_half",
    )(half, a, *before)


def unpack(half, blocks):
    count = len(ABOVE[half])
    low_rows = lax.broadcasted_iota(jnp.int32, (B, B), 0) >= H
    left = lax.broadcasted_iota(jnp.int32, (B, B), 1) < H
    guests = [block[H:] for block in blocks[count:]]
    upper = jnp.where(left[:H], guests[0], pltpu.roll(guests[1], H, 1))
    last = jnp.concatenate([upper, pltpu.roll(guests[2], H, 1)], axis=0)
    for pair, block in zip(ABOVE[half], blocks):
        yield pair, block
    for pair, block in zip(DIAGONAL[half], list(blocks[count:]) + [last]):
        yield pair, jnp.where(low_rows & left, block.T, block)


def inverse_factor(gram, width=4):
    k = gram.shape[0]
    rows = k // 8
    wide = jnp.concatenate([gram, jnp.zeros((k, B - k), jnp.float32)], axis=1)
    tiles = [wide[8 * t:8 * t + 8, :] for t in range(rows)]
    lane = lax.broadcasted_iota(jnp.int32, (8, B), 1)
    sub = lax.broadcasted_iota(jnp.int32, (8, B), 0)

    def row_of(tile, s):
        return jnp.broadcast_to(tile[s:s + 1, :], (8, B))

    def columns(start, first):
        return [
            {u: jnp.broadcast_to(tiles[u][:, c:c + 1], (8, B)) for u in range(first, rows)}
            for c in range(start, min(start + width, k))
        ]

    scale = [None] * rows
    now = columns(0, 0)
    for start in range(0, k, width):
        t, top = divmod(start, 8)
        ahead = columns(start + width, t)
        inside = (lane >= start) & (lane < start + width)
        unit = jnp.where(lane == sub + 8 * t, 1.0, 0.0)
        tiles[t] = jnp.where(inside & (sub >= top), unit, tiles[t])
        n = len(now)
        own = {(a, b): row_of(now[b][t], top + a) for a in range(n) for b in range(a + 1)}
        inverse, lower = [], {}
        for c in range(n):
            inverse.append(1.0 / own[c, c])
            root = lax.rsqrt(own[c, c])
            scale[t] = root if top + c == 0 else jnp.where(sub == top + c, root, scale[t])
            for a in range(c + 1, n):
                lower[a, c] = own[a, c] * inverse[c]
                for b in range(c + 1, a + 1):
                    own[a, b] = own[a, b] - lower[a, c] * own[b, c]
        ratios, lines = [], []
        for c in range(n):
            for o in range(c + 1, n):
                now[o][t] = now[o][t] - now[c][t] * lower[o, c]
            ratios.append([row_of(other[t], top + c) * inverse[c] for other in ahead])
            lines.append(row_of(tiles[t], top + c) * inverse[c])
            for other, ratio in zip(ahead, ratios[c]):
                other[t] = other[t] - now[c][t] * ratio
            tiles[t] = tiles[t] - jnp.where(sub > top + c, now[c][t], 0.0) * lines[c]
        for u in range(t + 1, rows):
            tiles[u] = jnp.where(inside, 0.0, tiles[u])
            for c in range(n):
                for o in range(c + 1, n):
                    now[o][u] = now[o][u] - now[c][u] * lower[o, c]
                for other, ratio in zip(ahead, ratios[c]):
                    other[u] = other[u] - now[c][u] * ratio
                tiles[u] = tiles[u] - now[c][u] * lines[c]
        now = ahead
    out = [jnp.where(lane <= sub + 8 * t, tiles[t], 0.0) * scale[t] for t in range(rows)]
    return jnp.concatenate(out, axis=0)[:, :k]


def times_gram(xt, parts):
    k, d = xt.shape
    p = -(-k // 16) * 16
    padded = jnp.concatenate([xt, jnp.zeros((p - k, d), jnp.float32)], axis=0)
    stack = jnp.concatenate(split(padded), axis=0)
    high = part_dot(stack, parts[0][...])
    mid = part_dot(stack[:2 * p], parts[1][...])
    low = part_dot(stack[:p], parts[2][...])
    out = (low + mid[p:] + high[2 * p:]) + (mid[:p] + high[p:2 * p]) + high[:p]
    return out[:k]


def fill_parts(half, packed, parts):
    blocks = [block_of(packed, index) for index in range(PACKED)]
    for (i, j), block in unpack(half, blocks):
        for part, value in zip(parts, split(block)):
            part[i * B:(i + 1) * B, j * B:(j + 1) * B] = value
        if i < j:
            for part, value in zip(parts, split(block.T)):
                part[j * B:(j + 1) * B, i * B:(i + 1) * B] = value


def iterate_kernel(total, core_ref, own_ref, other_ref, xt_ref, a_ref, rowt_ref, proj_ref, *parts):
    first = core_ref[0] == 0
    fill_parts(0, jnp.where(first, own_ref[...], other_ref[...]), parts)
    fill_parts(1, jnp.where(first, other_ref[...], own_ref[...]), parts)
    root = math.sqrt(total)
    xt = xt_ref[...]
    zt = times_gram(xt, parts)
    for step in range(ITERS + 1):
        gram = dot(xt, zt, NT)
        if step == ITERS:
            yt = dot(xt, a_ref[...], NT)
        inv = inverse_factor(gram)
        crosst = dot(inv, zt)
        if step == ITERS:
            break
        square = dot(crosst, crosst, NT)
        if step == 0:
            ahead = times_gram(crosst, parts)
        inv = inverse_factor(square)
        xt = dot(inv, crosst)
        zt = dot(inv, ahead) if step == 0 else times_gram(xt, parts)
    proj_ref[...] = crosst / root
    rowt_ref[...] = dot(inv, yt) * root


def iterate(total, core, own, other, xt, a):
    k, d = xt.shape
    vmem = pl.BlockSpec(memory_space=pltpu.VMEM)
    return pl.pallas_call(
        functools.partial(iterate_kernel, total),
        out_shape=(
            jax.ShapeDtypeStruct((k, a.shape[0]), jnp.float32),
            jax.ShapeDtypeStruct((k, d), jnp.float32),
        ),
        in_specs=[pl.BlockSpec(memory_space=pltpu.SMEM)] + [vmem] * 4,
        out_specs=(vmem, vmem),
        scratch_shapes=[pltpu.VMEM((d, d), jnp.bfloat16)] * 3,
        compiler_params=pltpu.CompilerParams(vmem_limit_bytes=32 * 1024 * 1024),
        name="iterate",
    )(core, own, other, xt, a)


def scatter_sum(v, axes):
    v = v.reshape(lax.axis_size(axes), -1, B)
    return jnp.sum(lax.all_to_all(v, axes, 0, 0, tiled=True), axis=0)


def collect(v, axes):
    copies = jnp.broadcast_to(v[None], (lax.axis_size(axes),) + v.shape)
    return lax.all_to_all(copies, axes, 0, 0, tiled=True)


def all_sum(v):
    v = scatter_sum(v, NEAR)
    for axes in FAR:
        v = jnp.sum(collect(v, axes), axis=0)
    return collect(v, NEAR).reshape(-1, B)


def swap(v):
    return lax.ppermute(v, "core", [(0, 1), (1, 0)])


def local(total, slab, test_matrix):
    core = lax.axis_index("core").astype(jnp.int32)[None]
    there = swap(slab)
    own = all_sum(gram_half(core, there, gram_half(core, slab)))
    rowt, projected = iterate(total, core, own, swap(own), test_matrix.T, slab)
    return rowt.T, projected


def solution(mesh):
    fine = Mesh(mesh.devices.reshape(4, 2, 4, 2, 2, 4), AXES)
    rows = P(AXES, None)

    def run(slab, test_matrix):
        return jax.shard_map(
            functools.partial(local, slab.shape[0]),
            mesh=fine,
            in_specs=(rows, P()),
            out_specs=(rows, P()),
            check_vma=False,
        )(slab, test_matrix)

    return run
```
